512 devices in a mesh: node: 32 (over x, y), head: 16 (over z, core).
Axes of the slice: x: 4, y: 8, z: 8, core: 2. Of those that a mesh axis runs over, the one named last changes fastest.
Arguments:
- states: bfloat16 [256, 5376], P(None, 'node'), may hold values from -24 to 24
- w_query: bfloat16 [5376, 4096], P('node', 'head'), may hold values from -0.078125 to 0.078125
- w_key_value: bfloat16 [5376, 4096], P('node', 'head'), may hold values from -0.078125 to 0.078125
- w_out: bfloat16 [4096, 5376], P('head', 'node'), may hold values from -9 to 9
- post_gain: float32 [5376], P('node'), may hold values from 0.5 to 1.5
- cache: bfloat16 [3072, 64, 16, 256], P('node', None, 'head'), may hold values from -244 to 244
- tails: bfloat16 [256, 64, 16, 256], P('node', None, 'head'), may hold values from -6 to 6
- lengths: int32 [256], P('node'), may hold values from 0 to 63, as said below
- ancestry: int32 [256, 128], replicated, may hold values from 0 to 1, as said below
- block_node: int32 [3072], P('node'), may hold values from 0 to 127, as said below
- matching: int32 [1024], replicated, may hold values from 0 to 255, as said below
Outputs:
- branch: bfloat16 [256, 5376], P('head', 'node')
- children: bfloat16 [1024, 64, 16, 256], P('node', None, 'head')
The draws below stay inside these ranges and needn't reach their ends.
Inputs may be any that keep to these rules, and one draw needn't show every extreme that they name: `lengths`: some leaf has 0 and some has 63. `ancestry`: row l marks the path from node 0, the shared prompt, to the node of leaf l, both ends included. `block_node`: node 0 is the shared prompt. `matching`: leaf l is homed on node index l // 8; the 32 children on one node index copy from leaves of exactly 32 node indices, exactly one child from each.
All inputs are finite; a program needn't handle non-finite values.
Results may differ from the reference program's by a relative error of at most 0.0095.
The reference program's roundings to bfloat16 on the way count: a program that leaves them out, or rounds other values in their place, can miss the bound.
Values may be sent and summed in bfloat16 or wider, within the bound.
No kernel may reach another device: no remote copies, remote signals or barrier semaphores. Data moves between devices by JAX's collectives and lax.ppermute only.
A program may use at most 64 MiB of HBM per device.

```python
import math
import jax
import jax.numpy as jnp
from jax import lax

D = 5376
HEADS = 32
KVH = 16
HD = 128
BLK = 64
NODES = 128
LEAF_DEV = 8
NB_DEV = 96
LEAVES = 256
NBLOCKS = 3072
CH_DEV = 32
CAP = 1


def draw_states(key, part):
    key = jax.random.fold_in(key, 16)
    key_base = jax.random.fold_in(key, 0)
    values = jnp.clip(jax.random.normal(key_base, (LEAVES, D), jnp.float32), -6.0, 6.0)
    return values.astype(jnp.bfloat16)


def draw_w_out(key, part):
    key = jax.random.fold_in(key, 17)
    key_base, key_scale = jax.random.split(key)
    columns = jnp.arange(D, dtype=jnp.float32) / D
    ramp = 1.0 + 2.0 * columns
    scales = jnp.exp(jax.random.uniform(key_scale, (1, D), jnp.float32, 0.0, math.log(10.0))) * ramp[None, :]
    base = jnp.clip(jax.random.normal(key_base, (HEADS * HD, D), jnp.float32), -6.0, 6.0) * (HEADS * HD) ** (-0.5)
    return (base * scales).astype(jnp.bfloat16)


def draw_cache(key, part):
    key = jax.random.fold_in(key, 15)
    key_base = jax.random.fold_in(key, 0)
    values = jnp.clip(jax.random.normal(key_base, (NBLOCKS, BLK, KVH, 2 * HD), jnp.float32), -6.0, 6.0)
    return values.astype(jnp.bfloat16)


def draw_lengths(key, part):
    key = jax.random.fold_in(key, 12)
    key_base, key_long, key_short = jax.random.split(key, 3)
    values = jax.random.randint(key_base, (LEAVES,), 0, BLK)
    longest = jax.random.randint(key_long, (), 0, LEAVES)
    shortest = (longest + 1 + jax.random.randint(key_short, (), 0, LEAVES - 1)) % LEAVES
    values = values.at[longest].set(BLK - 1).at[shortest].set(0)
    return values.astype(jnp.int32)


def draw_ancestry(key, part):
    key = jax.random.fold_in(key, 13)
    key_parent, key_leaf = jax.random.split(key)
    node_ids = jnp.arange(NODES, dtype=jnp.int32)
    parents = jax.random.randint(key_parent, (NODES,), 0, jnp.maximum(node_ids, 1))
    table = (node_ids[:, None] == node_ids[None, :]).astype(jnp.int32)

    def climb(index, current):
        return jnp.maximum(current, current[parents])
    table = lax.fori_loop(0, NODES, climb, table)
    leaf_nodes = jax.random.randint(key_leaf, (LEAVES,), 0, NODES)
    return table[leaf_nodes].astype(jnp.int32)


def draw_block_node(key, part):
    key = jax.random.fold_in(key, 14)
    key_level, key_prompt, key_other = jax.random.split(key, 3)
    shards = NBLOCKS // NB_DEV
    level = jax.random.randint(key_level, (shards,), 0, 4)
    per_block = jnp.repeat(level, NB_DEV)
    prompt = jax.random.randint(key_prompt, (NBLOCKS,), 0, 8) < 2 * per_block
    others = jax.random.randint(key_other, (NBLOCKS,), 1, NODES)
    return jnp.where(prompt, 0, others).astype(jnp.int32)


def draw_matching(key, part):
    key = jax.random.fold_in(key, 11)
    devices = LEAVES // LEAF_DEV
    groups = CH_DEV // CAP
    device_keys = jax.random.split(key, devices)

    def one_device(device_key):
        key_order, key_shuffle, key_leaf = jax.random.split(device_key, 3)
        chosen = jax.random.permutation(key_order, devices)[:groups]
        sources = jax.random.permutation(key_shuffle, jnp.repeat(chosen, CAP))
        leaf_pick = jax.random.randint(key_leaf, (CH_DEV,), 0, LEAF_DEV)
        return sources * LEAF_DEV + leaf_pick
    return jax.vmap(one_device)(device_keys).reshape(-1).astype(jnp.int32)


def levels(own_key, extent, cuts, least, top_value):
    factor_of = 1.0
    for axis_at, shards_of in cuts:
        heights = jax.random.uniform(jax.random.fold_in(jax.random.fold_in(own_key, 6), axis_at), (shards_of,), jnp.float32, least / len(cuts), top_value / len(cuts))
        factor_of = factor_of * jnp.repeat(jnp.exp(heights), extent[axis_at] // shards_of).reshape((-1,) + (1,) * (len(extent) - 1 - axis_at))
    return factor_of


def noise(own_key, shape, spread, reach, pieces=(), kind=jnp.bfloat16):
    factor_of = levels(own_key, shape, pieces, -0.22, 0.18) if pieces else 1.0
    values = jax.random.normal(own_key, shape, jnp.float32) * spread * factor_of
    return jnp.minimum(jnp.maximum(values, -reach), reach).astype(kind)


def setup_inputs(seed: int = 0) -> dict:
    streams_of = jax.random.split(jax.random.key(seed), 12)
    return {
        "states": draw_states(jax.random.fold_in(streams_of[11], 71), 0),
        "w_query": noise(streams_of[1], (D, HEADS * HD), D ** -0.5, 0.078125, ((0, 32), (1, 16))),
        "w_key_value": noise(streams_of[2], (D, KVH * 2 * HD), D ** -0.5, 0.078125, ((0, 32), (1, 16))),
        "w_out": draw_w_out(jax.random.fold_in(streams_of[11], 71), 0),
        "post_gain": jnp.clip(1.0 + 0.1 * jax.random.normal(streams_of[4], (D,), jnp.float32), 0.5, 1.5),
        "cache": draw_cache(jax.random.fold_in(streams_of[11], 71), 0),
        "tails": noise(streams_of[6], (LEAVES, BLK, KVH, 2 * HD), 1.0, 6.0, ((0, 32), (2, 16))),
        "lengths": draw_lengths(jax.random.fold_in(streams_of[11], 71), 0),
        "ancestry": draw_ancestry(jax.random.fold_in(streams_of[11], 71), 0),
        "block_node": draw_block_node(jax.random.fold_in(streams_of[11], 71), 0),
        "matching": draw_matching(jax.random.fold_in(streams_of[11], 71), 0),
    }


score_scale = 168.0 ** (-0.5)
epsilon = 1e-06

def head_attention(query_head, cache_head, tail_head, fresh_head, visible_keys, live_rows):
    group_q = query_head.shape[1]
    query_f = query_head.astype(jnp.float32)
    flat_query = query_f.reshape(-1, HD)
    cache_flat = cache_head.reshape(-1, 2 * HD).astype(jnp.float32)
    scores = jnp.dot(flat_query, cache_flat[:, :HD].T, preferred_element_type=jnp.float32) * score_scale
    keep_mask = jnp.repeat(visible_keys, group_q, axis=0)
    tail_f = tail_head.astype(jnp.float32)
    tail_scores = jnp.einsum('lgd,lrd->lgr', query_f, tail_f[..., :HD]) * score_scale
    tail_keep = live_rows[:, None, :]
    fresh_f = fresh_head.astype(jnp.float32)
    self_scores = lax.optimization_barrier(jnp.sum(query_f * fresh_f[:, None, :HD], axis=-1)) * score_scale
    row_max = lax.optimization_barrier(jnp.max(jnp.where(keep_mask, scores, -jnp.inf), axis=1)).reshape(-1, group_q)
    row_max = jnp.maximum(row_max, lax.optimization_barrier(jnp.max(jnp.where(tail_keep, tail_scores, -jnp.inf), axis=-1)))
    row_max = jnp.maximum(row_max, self_scores)
    flat_max = row_max.reshape(-1)
    weights = jnp.where(keep_mask, jnp.exp(scores - flat_max[:, None]), 0.0).astype(jnp.bfloat16)
    denominator = lax.optimization_barrier(jnp.sum(weights.astype(jnp.float32), axis=1))
    output = jnp.dot(weights.astype(jnp.float32), cache_flat[:, HD:], preferred_element_type=jnp.float32)
    tail_weights = jnp.where(tail_keep, jnp.exp(tail_scores - row_max[..., None]), 0.0).astype(jnp.bfloat16)
    self_weights = jnp.exp(self_scores - row_max).astype(jnp.bfloat16)
    denominator = denominator.reshape(-1, group_q) + lax.optimization_barrier(jnp.sum(tail_weights.astype(jnp.float32), axis=-1))
    denominator = denominator + self_weights.astype(jnp.float32)
    output = output.reshape(-1, group_q, HD) + jnp.einsum('lgr,lrd->lgd', tail_weights.astype(jnp.float32), tail_f[..., HD:])
    output = output + self_weights.astype(jnp.float32)[..., None] * fresh_f[:, None, HD:]
    return output / denominator[..., None]

def reference(states, w_query, w_key_value, w_out, post_gain, cache, tails, lengths, ancestry, block_node, matching):
    query = jnp.dot(states, w_query, preferred_element_type=jnp.float32).astype(jnp.bfloat16)
    fresh = jnp.dot(states, w_key_value, preferred_element_type=jnp.float32).astype(jnp.bfloat16)
    query = query.reshape(LEAVES, KVH, HEADS // KVH, HD)
    fresh = fresh.reshape(LEAVES, KVH, 2 * HD)
    visible = ancestry[:, block_node] > 0
    visible_keys = jnp.repeat(visible, BLK, axis=1)
    live_rows = jnp.arange(BLK, dtype=jnp.int32)[None, :] < lengths[:, None]

    def one_head(head_id):
        query_head = lax.dynamic_index_in_dim(query, head_id, axis=1, keepdims=False)
        cache_head = lax.dynamic_index_in_dim(cache, head_id, axis=2, keepdims=False)
        tail_head = lax.dynamic_index_in_dim(tails, head_id, axis=2, keepdims=False)
        fresh_head = lax.dynamic_index_in_dim(fresh, head_id, axis=1, keepdims=False)
        return head_attention(query_head, cache_head, tail_head, fresh_head, visible_keys, live_rows)
    per_head = lax.map(one_head, jnp.arange(KVH, dtype=jnp.int32))
    attention = per_head.transpose(1, 0, 2, 3).reshape(LEAVES, HEADS * HD).astype(jnp.bfloat16)
    projected = jnp.dot(attention, w_out, preferred_element_type=jnp.float32)
    mean_square = lax.optimization_barrier(jnp.mean(projected * projected, axis=1))
    branch = (projected * lax.rsqrt(mean_square + epsilon)[:, None] * post_gain[None, :]).astype(jnp.bfloat16)
    row_ids = jnp.arange(BLK, dtype=jnp.int32)[None, :, None, None]
    limit_rows = lengths[:, None, None, None]
    updated = jnp.where(row_ids < limit_rows, tails, jnp.where(row_ids == limit_rows, fresh[:, None], jnp.zeros_like(tails)))
    children = updated[matching]
    return (branch, children)
```

```python
import functools
import math

import jax
import jax.numpy as jnp
from jax import lax
from jax.experimental import pallas as pl
from jax.experimental.pallas import tpu as pltpu
from jax.sharding import PartitionSpec as P

D = 5376
HEADS = 32
KVH = 16
HD = 128
BLK = 64
GROUP = HEADS // KVH

score_scale = 168.0 ** (-0.5)
log2_scale = score_scale * math.log2(math.e)
neg_big = -1e30
epsilon = 1e-06
f32 = jnp.float32
bf16 = jnp.bfloat16
CHUNK = 1024
VROWS = HD + 16

VMEM = pl.BlockSpec(memory_space=pltpu.VMEM)
SMEM = pl.BlockSpec(memory_space=pltpu.SMEM)
HBM = pl.BlockSpec(memory_space=pltpu.HBM)


def call(kernel, out_shape, in_specs, out_specs, scratch=(), vmem=8, cost=(0, 0, 0)):
    return pl.pallas_call(
        kernel,
        out_shape=out_shape,
        in_specs=in_specs,
        out_specs=out_specs,
        scratch_shapes=list(scratch),
        compiler_params=pltpu.CompilerParams(vmem_limit_bytes=vmem * 1024 * 1024),
        cost_estimate=pl.CostEstimate(flops=cost[0], bytes_accessed=cost[1], transcendentals=cost[2]),
    )


def matmul_nt(a, b):
    return lax.dot_general(a, b, (((1,), (1,)), ((), ())), preferred_element_type=f32)


def identity(size):
    rows = lax.broadcasted_iota(jnp.int32, (size, size), 0)
    cols = lax.broadcasted_iota(jnp.int32, (size, size), 1)
    return (rows == cols).astype(f32).astype(bf16)


def project_kernel(states_hbm, query_hbm, key_value_hbm, out, states_t, w_query, w_key_value, sems):
    pairs = ((states_hbm, states_t), (query_hbm, w_query), (key_value_hbm, w_key_value))
    copies = [pltpu.make_async_copy(pair[0], pair[1], sems.at[i]) for i, pair in enumerate(pairs)]
    for copy in copies:
        copy.start()
    dims = (((0,), (0,)), ((), ()))
    cols = w_query.shape[1]
    copies[0].wait()
    copies[1].wait()
    out[:, :cols] = lax.dot_general(states_t[...], w_query[...], dims, preferred_element_type=f32)
    copies[2].wait()
    out[:, cols:] = lax.dot_general(states_t[...], w_key_value[...], dims, preferred_element_type=f32)


def home_kernel(parts, rows_rep, fresh):
    total = jnp.sum(parts[...], axis=0)
    pair = jnp.concatenate([total, total], axis=0).astype(bf16)
    for index in range(rows_rep.shape[0] // 16):
        rows_rep[pl.ds(index * 16, 16), :] = pair
    fresh[...] = total[:, total.shape[1] // 2 :]


def attend_kernel(
    rows_hbm,
    cache_hbm,
    tails_hbm,
    fresh_hbm,
    ancestry_hbm,
    block_node_hbm,
    lengths_hbm,
    out,
    scores,
    values_t,
    updated,
    bias,
    cache,
    queries,
    tails,
    fresh,
    ancestry,
    block_node,
    lengths,
    sems,
):
    node = lax.axis_index("node")
    leaves = queries.shape[0]
    cached = cache.shape[0]
    steps = range(0, cached, CHUNK)
    pairs = [
        (ancestry_hbm, ancestry),
        (block_node_hbm, block_node),
        (lengths_hbm, lengths),
        (tails_hbm, tails),
        (fresh_hbm, fresh),
        (rows_hbm.at[:, pl.ds(0, queries.shape[1])], queries),
    ]
    pairs += [(cache_hbm.at[pl.ds(start, CHUNK), :], cache.at[pl.ds(start, CHUNK), :]) for start in steps]
    copies = [pltpu.make_async_copy(pair[0], pair[1], sems.at[i]) for i, pair in enumerate(pairs)]
    for copy in copies:
        copy.start()
    for copy in copies[:2]:
        copy.wait()
    nodes_all = ancestry.shape[1]
    tree = lax.broadcasted_iota(jnp.int32, (nodes_all, block_node.shape[1]), 0)
    one_hot = (tree == block_node[...]).astype(f32).astype(bf16)
    seen = lax.dot_general(
        one_hot,
        ancestry[...].astype(f32).astype(bf16),
        (((0,), (1,)), ((), ())),
        preferred_element_type=f32,
    )
    shut = jnp.where(seen > 0.5, 0.0, neg_big)
    for g in range(GROUP):
        bias[:, g * leaves : (g + 1) * leaves] = shut
    eye = identity(HD)
    values_t[HD:, :] = jnp.ones((VROWS - HD, values_t.shape[1]), bf16)
    for copy in copies[2:5]:
        copy.wait()
    leaf_dev = fresh.shape[0]
    lanes = lax.broadcasted_iota(jnp.int32, lengths.shape, 1)
    length = [
        jnp.sum(jnp.where(lanes == leaf, lengths[...], 0).astype(f32), axis=1, keepdims=True)
        for leaf in range(leaf_dev)
    ]
    rows = lax.broadcasted_iota(jnp.int32, (BLK, 2 * HD), 0).astype(f32)
    for leaf in range(leaf_dev):
        span = pl.ds(leaf * BLK, BLK)
        block = jnp.where(rows < length[leaf], tails[span, :].astype(f32), 0.0)
        block = jnp.where(rows == length[leaf], fresh[leaf : leaf + 1, :], block)
        updated[span, :] = block.astype(bf16)
    values_t[:HD, cached:] = matmul_nt(eye, updated[:, HD:]).astype(bf16)
    rows_all = leaves * GROUP
    copies[5].wait()
    query = jnp.concatenate([queries[:, HD * g : HD * (g + 1)] for g in range(GROUP)], axis=0)
    own = updated.shape[0]
    top = jnp.full((8, rows_all), neg_big, f32)
    lanes = lax.broadcasted_iota(jnp.int32, (BLK, rows_all), 1) % leaves
    rows = lax.broadcasted_iota(jnp.int32, (BLK, rows_all), 0).astype(f32)
    raw = matmul_nt(updated[:, :HD], query)
    for leaf in range(leaf_dev):
        keep = (lanes == node * leaf_dev + leaf) & (rows <= length[leaf])
        part = jnp.where(keep, raw[leaf * BLK : (leaf + 1) * BLK] * log2_scale, neg_big)
        scores[pl.ds(cached + leaf * BLK, BLK), :] = part
        top = jnp.maximum(top, jnp.max(part.reshape(BLK // 8, 8, rows_all), axis=0))
    for step, start in enumerate(steps):
        copies[6 + step].wait()
        values_t[:HD, start : start + CHUNK] = matmul_nt(eye, cache[start : start + CHUNK, HD:]).astype(bf16)
        raw = matmul_nt(cache[start : start + CHUNK, :HD], query)
        for block in range(CHUNK // BLK):
            at = start // BLK + block
            part = raw[block * BLK : (block + 1) * BLK] * log2_scale + bias[at : at + 1, :]
            scores[pl.ds(start + block * BLK, BLK), :] = part
            top = jnp.maximum(top, jnp.max(part.reshape(BLK // 8, 8, rows_all), axis=0))
    row_max = jnp.max(top, axis=0, keepdims=True)
    total = jnp.zeros((VROWS, rows_all), f32)
    for start in range(0, cached + own, CHUNK):
        stop = min(start + CHUNK, cached + own)
        weights = jnp.exp2(scores[start:stop, :] - row_max).astype(bf16)
        total = total + jnp.dot(values_t[:, start:stop], weights, preferred_element_type=f32)
    weight_sum = total[HD : HD + 1]
    mean_t = (total[:HD] / weight_sum).astype(bf16)
    level = row_max + jnp.log2(weight_sum)
    high = level.astype(bf16).astype(f32)
    middle = (level - high).astype(bf16).astype(f32)
    low = level - high - middle
    index = lax.broadcasted_iota(jnp.int32, (HD, rows_all), 0)
    level_t = jnp.where(index == 0, high, jnp.where(index == 1, middle, jnp.where(index == 2, low, 0.0)))
    for leaf in range(leaf_dev):
        level_t = jnp.where(index == 3 + leaf, length[leaf], level_t)
    level_t = level_t.astype(bf16)
    eye = identity(leaves)
    nodes = out.shape[0]
    for part, array in enumerate((mean_t, level_t)):
        turned = [
            matmul_nt(eye, array[:, g * leaves : (g + 1) * leaves]).reshape(nodes, leaf_dev, HD)
            for g in range(GROUP)
        ]
        span = GROUP * leaf_dev
        out[:, part * span : (part + 1) * span, :] = jnp.concatenate(turned, axis=1).astype(bf16)


def combine_kernel(parts, out):
    span = parts.shape[1] // 2
    mean = parts[:, :span, :].astype(f32)
    level = parts[:, span:, :].astype(f32)
    lanes = lax.broadcasted_iota(jnp.int32, level.shape, 2)
    level = jnp.sum(jnp.where(lanes < 3, level, 0.0), axis=2, keepdims=True)
    top = jnp.max(level, axis=0, keepdims=True)
    weight = jnp.broadcast_to(jnp.exp2(level - top), mean.shape)
    result = jnp.sum(weight * mean, axis=0) / jnp.sum(weight, axis=0)
    leaf_dev = span // GROUP
    mine = jnp.concatenate([result[g * leaf_dev : (g + 1) * leaf_dev] for g in range(GROUP)], axis=1)
    pair = jnp.concatenate([mine, mine], axis=0).astype(bf16)
    for index in range(out.shape[0] // 16):
        out[pl.ds(index * 16, 16), :] = pair


def output_kernel(attention, w_out_t, partial):
    partial[...] = matmul_nt(attention[...], w_out_t[...]).astype(bf16)


def square_kernel(partial, projected, squares):
    total = jnp.sum(partial[...].astype(f32), axis=0)
    projected[...] = total
    sums = jnp.sum(total * total, axis=1, keepdims=True)
    leaves = total.shape[0]
    rows = lax.broadcasted_iota(jnp.int32, (leaves, HD), 0)
    cols = lax.broadcasted_iota(jnp.int32, (leaves, HD), 1)
    line = jnp.sum(jnp.where(rows == cols, sums, 0.0), axis=0, keepdims=True)
    squares[...] = jnp.broadcast_to(line, squares.shape)


def scale_kernel(squares, projected, gain, branch):
    leaves = projected.shape[0]
    line = jnp.sum(squares[...], axis=0, keepdims=True)
    rows = lax.broadcasted_iota(jnp.int32, (leaves, HD), 0)
    cols = lax.broadcasted_iota(jnp.int32, (leaves, HD), 1)
    sums = jnp.sum(jnp.where(rows == cols, line, 0.0), axis=1, keepdims=True)
    inverse = lax.rsqrt(sums / D + epsilon)
    branch[...] = (projected[...] * inverse * gain[...]).astype(bf16)


def children_kernel(leaf_dev, sources, tails, rows_all, levels, out, blocks, fresh, lens, sems):
    count = out.shape[0]
    copies = []
    for index in range(count):
        copy = pltpu.make_async_copy(tails.at[sources[index]], blocks.at[index], sems.at[index])
        copy.start()
        copies.append(copy)
    span = levels.shape[1] // 2
    fresh[...] = rows_all[:, rows_all.shape[1] // 2 :].astype(f32)
    lens[...] = jnp.max(levels[:, span:, :].astype(f32), axis=1)
    rows = lax.broadcasted_iota(jnp.int32, (BLK, 2 * HD), 0).astype(f32)
    lanes = lax.broadcasted_iota(jnp.int32, (1, HD), 1)
    for index in range(count):
        leaf = sources[index]
        line = lens[pl.ds(leaf // leaf_dev, 1), :]
        length = jnp.sum(jnp.where(lanes == 3 + leaf % leaf_dev, line, 0.0), axis=1, keepdims=True)
        copies[index].wait()
        block = jnp.where(rows < length, blocks[index].astype(f32), 0.0)
        block = jnp.where(rows == length, fresh[pl.ds(leaf, 1), :], block)
        out[index] = block.astype(bf16)


def shards(
    states,
    w_query,
    w_key_value,
    w_out,
    post_gain,
    cache,
    tails,
    lengths,
    ancestry,
    block_node,
    matching,
):
    nodes = lax.axis_size("node")
    heads = lax.axis_size("head")
    node = lax.axis_index("node")
    leaves = states.shape[0]
    leaf_dev = leaves // nodes
    query_cols = w_query.shape[1]
    all_cols = query_cols + w_key_value.shape[1]
    columns = w_out.shape[1]
    rows_all = leaves * GROUP
    child_dev = matching.shape[0] // nodes
    shape = jax.ShapeDtypeStruct

    cache_rows = cache.reshape(-1, 2 * HD)
    tail_rows = tails.reshape(-1, 2 * HD)
    key_count = cache_rows.shape[0]
    extended = key_count + leaf_dev * BLK
    all_tails = lax.all_gather(tail_rows, "node", axis=0, tiled=True)

    partial = call(
        project_kernel,
        shape((leaves, all_cols), f32),
        [HBM] * 3,
        VMEM,
        [
            pltpu.VMEM((states.shape[1], leaves), bf16),
            pltpu.VMEM(w_query.shape, bf16),
            pltpu.VMEM(w_key_value.shape, bf16),
            pltpu.SemaphoreType.DMA((3,)),
        ],
        vmem=60,
        cost=(2 * leaves * all_cols * states.shape[1], 1000000, 0),
    )(states.T, w_query, w_key_value)
    parts = lax.all_to_all(partial.reshape(nodes, leaf_dev, all_cols), "node", 0, 0, tiled=True)

    rows_rep, fresh = call(
        home_kernel,
        (shape((leaves, all_cols), bf16), shape((leaf_dev, 2 * HD), f32)),
        [VMEM],
        (VMEM, VMEM),
        cost=(leaves * all_cols, 4 * leaves * all_cols, 0),
    )(parts)
    rows = lax.all_to_all(rows_rep.reshape(nodes, leaf_dev, all_cols), "node", 0, 0, tiled=True)
    rows = rows.reshape(leaves, all_cols)
    span = 2 * GROUP * leaf_dev
    sent = call(
        attend_kernel,
        shape((nodes, span, HD), bf16),
        [HBM] * 7,
        VMEM,
        [
            pltpu.VMEM((extended, rows_all), f32),
            pltpu.VMEM((VROWS, extended), bf16),
            pltpu.VMEM((leaf_dev * BLK, 2 * HD), bf16),
            pltpu.VMEM((block_node.shape[0], rows_all), f32),
            pltpu.VMEM(cache_rows.shape, bf16),
            pltpu.VMEM((leaves, query_cols), bf16),
            pltpu.VMEM(tail_rows.shape, bf16),
            pltpu.VMEM(fresh.shape, f32),
            pltpu.VMEM(ancestry.shape, jnp.int32),
            pltpu.VMEM((1, block_node.shape[0]), jnp.int32),
            pltpu.VMEM((1, leaf_dev), jnp.int32),
            pltpu.SemaphoreType.DMA((6 + key_count // CHUNK,)),
        ],
        vmem=60,
        cost=(4 * rows_all * extended * HD, 8 * HD * key_count, rows_all * extended),
    )(
        rows,
        cache_rows,
        tail_rows,
        fresh,
        ancestry,
        block_node.reshape(1, -1),
        lengths.reshape(1, -1),
    )
    landed = lax.all_to_all(sent, "node", 0, 0, tiled=True)
    mine = call(
        combine_kernel,
        shape((leaves, query_cols), bf16),
        [VMEM],
        VMEM,
        cost=(10 * rows_all * HD, 4 * rows_all * HD, rows_all * HD),
    )(landed)
    attention = lax.all_to_all(mine.reshape(nodes, leaf_dev, query_cols), "node", 0, 0, tiled=True)
    leaf_out = leaves // heads
    partial_out = call(
        output_kernel,
        shape((leaves, columns), bf16),
        [VMEM, VMEM],
        VMEM,
        cost=(2 * leaves * columns * query_cols, 6 * columns * query_cols, 0),
    )(attention.reshape(leaves, query_cols), w_out.T)
    partial_out = lax.all_to_all(
        partial_out.reshape(heads, leaf_out, columns), "head", 0, 0, tiled=True
    )
    projected, squares = call(
        square_kernel,
        (shape((leaf_out, columns), f32), shape((nodes, HD), f32)),
        [VMEM],
        (VMEM, VMEM),
        cost=(leaves * columns, 4 * leaves * columns, 0),
    )(partial_out)
    squares = lax.all_to_all(squares.reshape(nodes, 1, HD), "node", 0, 0, tiled=True)
    sources = lax.dynamic_slice_in_dim(matching, node * child_dev, child_dev, 0)
    children = call(
        functools.partial(children_kernel, leaf_dev),
        shape((child_dev, BLK, 2 * HD), bf16),
        [SMEM, HBM, VMEM, VMEM],
        VMEM,
        [
            pltpu.VMEM((child_dev, BLK, 2 * HD), bf16),
            pltpu.VMEM((leaves, 2 * HD), f32),
            pltpu.VMEM((nodes, HD), f32),
            pltpu.SemaphoreType.DMA((child_dev,)),
        ],
        vmem=60,
        cost=(1000000, 4 * child_dev * BLK * 2 * HD, 0),
    )(sources, all_tails.reshape(leaves, BLK, 2 * HD), rows, landed)
    squares, children = lax.optimization_barrier((squares, children))
    branch = call(
        scale_kernel,
        shape((leaf_out, columns), bf16),
        [VMEM] * 3,
        VMEM,
    )(squares.reshape(nodes, HD), projected, post_gain.reshape(1, columns))
    return (branch, children.reshape(child_dev, BLK, 1, 2 * HD))


def solution(mesh):
    return jax.shard_map(
        shards,
        mesh=mesh,
        in_specs=(
            P(None, "node"),
            P("node", "head"),
            P("node", "head"),
            P("head", "node"),
            P("node"),
            P("node", None, "head", None),
            P("node", None, "head", None),
            P("node"),
            P(),
            P("node"),
            P(),
        ),
        out_specs=(P("head", "node"), P("node", None, "head", None)),
        check_vma=False,
    )
```

```python
import math

import jax
import jax.numpy as jnp
from jax import lax
from jax.experimental import pallas as pl
from jax.experimental.pallas import tpu as pltpu
from jax.sharding import PartitionSpec as P

D = 5376
HEADS = 32
KVH = 16
HD = 128
BLK = 64
GROUP = HEADS // KVH

score_scale = 168.0 ** (-0.5)
log2_scale = score_scale * math.log2(math.e)
neg_big = -1e30
epsilon = 1e-06
f32 = jnp.float32
bf16 = jnp.bfloat16
CHUNK = 3072
VROWS = HD + 16
FIRST = 56
SECOND = 8

VMEM = pl.BlockSpec(memory_space=pltpu.VMEM)
SMEM = pl.BlockSpec(memory_space=pltpu.SMEM)
HBM = pl.BlockSpec(memory_space=pltpu.HBM)


def call(kernel, out_shape, in_specs, out_specs, scratch=(), vmem=8, cost=(0, 0, 0)):
    return pl.pallas_call(
        kernel,
        out_shape=out_shape,
        in_specs=in_specs,
        out_specs=out_specs,
        scratch_shapes=list(scratch),
        compiler_params=pltpu.CompilerParams(vmem_limit_bytes=vmem * 1024 * 1024),
        cost_estimate=pl.CostEstimate(flops=cost[0], bytes_accessed=cost[1], transcendentals=cost[2]),
    )


def matmul_nt(a, b):
    return lax.dot_general(a, b, (((1,), (1,)), ((), ())), preferred_element_type=f32)


def identity(size):
    rows = lax.broadcasted_iota(jnp.int32, (size, size), 0)
    cols = lax.broadcasted_iota(jnp.int32, (size, size), 1)
    return (rows == cols).astype(f32).astype(bf16)


def halves(value):
    high = value.astype(bf16)
    return high, (value - high.astype(f32)).astype(bf16)


def project_kernel(
    states_hbm, query_hbm, key_value_hbm, matching_hbm, out, picks, states_t, w_query, w_key_value, matching, sems
):
    pairs = (
        (states_hbm, states_t),
        (query_hbm, w_query),
        (key_value_hbm, w_key_value),
        (matching_hbm, matching),
    )
    copies = [pltpu.make_async_copy(pair[0], pair[1], sems.at[i]) for i, pair in enumerate(pairs)]
    for copy in copies:
        copy.start()
    dims = (((0,), (0,)), ((), ()))
    cols = w_query.shape[1]
    copies[0].wait()
    copies[1].wait()
    query = lax.dot_general(states_t[...], w_query[...], dims, preferred_element_type=f32)
    out[:, :cols], out[:, cols : 2 * cols] = halves(query)
    copies[2].wait()
    fresh = lax.dot_general(states_t[...], w_key_value[...], dims, preferred_element_type=f32)
    key, rest = halves(fresh[:, :HD])
    out[:, 2 * cols :] = jnp.concatenate([key, rest, fresh[:, HD:].astype(bf16)], axis=1)
    copies[3].wait()
    node = lax.axis_index("node")
    child_dev = matching.shape[0] * HD // lax.axis_size("node")
    leaf_dev = states_t.shape[1] // lax.axis_size("node")
    parent = matching[...]
    first = node * leaf_dev
    own = (parent >= first) & (parent < first + leaf_dev)
    part = jnp.where(own, parent - first, 0).astype(f32).astype(bf16)
    of = lax.broadcasted_iota(jnp.int32, (HD, HD), 0) // child_dev
    to = lax.broadcasted_iota(jnp.int32, (HD, HD), 1) // child_dev
    same = (of == to).astype(f32).astype(bf16)
    picks[...] = jnp.dot(part, same, preferred_element_type=f32).astype(jnp.int32)


def home_kernel(
    parts_hbm,
    tails_hbm,
    lengths_hbm,
    picks_hbm,
    sends,
    updated,
    second,
    parts,
    tails,
    lengths,
    blocks,
    picks,
    sems,
):
    pairs = (
        (parts_hbm, parts),
        (lengths_hbm, lengths),
        (tails_hbm, tails),
        (picks_hbm, picks),
    )
    copies = [pltpu.make_async_copy(pair[0], pair[1], sems.at[i]) for i, pair in enumerate(pairs)]
    for copy in copies:
        copy.start()
    copies[1].wait()
    length = leaf_lengths(lengths)
    copies[0].wait()
    leaf_dev = lengths.shape[1]
    total = jnp.sum(parts[...].astype(f32).reshape(-1, leaf_dev, parts.shape[1]), axis=0)
    cols = GROUP * HD
    query = (total[:, :cols] + total[:, cols : 2 * cols]).astype(bf16).astype(f32)
    total = total[:, 2 * cols :]
    fresh = jnp.concatenate([total[:, :HD] + total[:, HD : 2 * HD], total[:, 2 * HD :]], axis=1)
    rows = lax.broadcasted_iota(jnp.int32, (BLK, 2 * HD), 0).astype(f32)
    copies[2].wait()
    for leaf in range(leaf_dev):
        span = pl.ds(leaf * BLK, BLK)
        block = jnp.where(rows < length[leaf], tails[span, :].astype(f32), 0.0)
        block = jnp.where(rows == length[leaf], fresh[leaf : leaf + 1], block)
        block = block.astype(bf16)
        updated[span, :] = block
        blocks[span, :] = block.astype(f32)
    copies[3].wait()
    for index in range(sends.shape[0]):
        start = pl.multiple_of(pick_of(picks, index, sends.shape[0]) * BLK, BLK)
        block = blocks[pl.ds(start, BLK), :]
        sends[index] = jnp.concatenate([query, block[:FIRST]], axis=0).astype(bf16)
        second[index] = jnp.concatenate([query, block[FIRST:]], axis=0).astype(bf16)


def pick_of(picks, index, count):
    line = HD * picks.shape[0] // count
    return picks[index * line // HD, index * line % HD]


def leaf_lengths(lengths):
    lanes = lax.broadcasted_iota(jnp.int32, lengths.shape, 1)
    return [
        jnp.sum(jnp.where(lanes == leaf, lengths[...], 0).astype(f32), axis=1, keepdims=True)
        for leaf in range(lengths.shape[1])
    ]


def attend_kernel(
    rows_hbm,
    cache_hbm,
    updated_hbm,
    ancestry_hbm,
    block_node_hbm,
    lengths_hbm,
    out,
    scores,
    values_t,
    updated,
    bias,
    cache,
    rows_in,
    ancestry,
    block_node,
    lengths,
    sems,
):
    node = lax.axis_index("node")
    nodes = rows_in.shape[0]
    leaf_dev = lengths.shape[1]
    leaves = nodes * leaf_dev
    cached = cache.shape[0]
    steps = range(0, cached, CHUNK)
    pairs = [
        (ancestry_hbm, ancestry),
        (block_node_hbm, block_node),
        (lengths_hbm, lengths),
        (updated_hbm, updated),
        (rows_hbm.at[:, pl.ds(0, rows_in.shape[1]), :], rows_in),
    ]
    pairs += [(cache_hbm.at[pl.ds(start, CHUNK), :], cache.at[pl.ds(start, CHUNK), :]) for start in steps]
    copies = [pltpu.make_async_copy(pair[0], pair[1], sems.at[i]) for i, pair in enumerate(pairs)]
    for copy in copies:
        copy.start()
    for copy in copies[:2]:
        copy.wait()
    nodes_all = ancestry.shape[1]
    tree = lax.broadcasted_iota(jnp.int32, (nodes_all, block_node.shape[1]), 0)
    one_hot = (tree == block_node[...]).astype(f32).astype(bf16)
    seen = lax.dot_general(
        one_hot,
        ancestry[...].astype(f32).astype(bf16),
        (((0,), (1,)), ((), ())),
        preferred_element_type=f32,
    )
    shut = jnp.where(seen > 0.5, 0.0, neg_big)
    for g in range(GROUP):
        bias[:, g * leaves : (g + 1) * leaves] = shut
    eye = identity(HD)
    values_t[HD:, :] = jnp.ones((VROWS - HD, values_t.shape[1]), bf16)
    for copy in copies[2:4]:
        copy.wait()
    length = leaf_lengths(lengths)
    values_t[:HD, cached:] = matmul_nt(eye, updated[:, HD:]).astype(bf16)
    rows_all = leaves * GROUP
    copies[4].wait()
    queries = rows_in[...].astype(f32)[:, :leaf_dev, :].reshape(leaves, GROUP * HD)
    query = jnp.concatenate([queries[:, HD * g : HD * (g + 1)] for g in range(GROUP)], axis=0)
    query = query.astype(bf16)
    own = updated.shape[0]
    top = jnp.full((8, rows_all), neg_big, f32)
    lanes = lax.broadcasted_iota(jnp.int32, (BLK, rows_all), 1) % leaves
    rows = lax.broadcasted_iota(jnp.int32, (BLK, rows_all), 0).astype(f32)
    raw = matmul_nt(updated[:, :HD], query)
    for leaf in range(leaf_dev):
        keep = (lanes == node * leaf_dev + leaf) & (rows <= length[leaf])
        part = jnp.where(keep, raw[leaf * BLK : (leaf + 1) * BLK] * log2_scale, neg_big)
        scores[pl.ds(cached + leaf * BLK, BLK), :] = part
        top = jnp.maximum(top, jnp.max(part.reshape(BLK // 8, 8, rows_all), axis=0))
    for step, start in enumerate(steps):
        copies[5 + step].wait()
        values_t[:HD, start : start + CHUNK] = matmul_nt(eye, cache[start : start + CHUNK, HD:]).astype(bf16)
        raw = matmul_nt(cache[start : start + CHUNK, :HD], query)
        for block in range(CHUNK // BLK):
            at = start // BLK + block
            part = raw[block * BLK : (block + 1) * BLK] * log2_scale + bias[at : at + 1, :]
            scores[pl.ds(start + block * BLK, BLK), :] = part
            top = jnp.maximum(top, jnp.max(part.reshape(BLK // 8, 8, rows_all), axis=0))
    row_max = jnp.max(top, axis=0, keepdims=True)
    total = jnp.zeros((VROWS, rows_all), f32)
    for start in range(0, cached + own, CHUNK):
        stop = min(start + CHUNK, cached + own)
        weights = jnp.exp2(scores[start:stop, :] - row_max).astype(bf16)
        total = total + jnp.dot(values_t[:, start:stop], weights, preferred_element_type=f32)
    weight_sum = total[HD : HD + 1]
    mean_t = (total[:HD] / weight_sum).astype(bf16)
    level = row_max + jnp.log2(weight_sum)
    high = level.astype(bf16).astype(f32)
    middle = (level - high).astype(bf16).astype(f32)
    low = level - high - middle
    lines = (nodes * 8, rows_all)
    line = lax.broadcasted_iota(jnp.int32, lines, 0)
    row = lax.broadcasted_iota(jnp.int32, lines, 1)
    part = line % 8
    level = jnp.where(part == 0, high, jnp.where(part == 1, middle, jnp.where(part == 2, low, 0.0)))
    level = jnp.where(row % leaves // leaf_dev == line // 8, level, 0.0).astype(bf16)
    row = lax.broadcasted_iota(jnp.int32, (rows_all, HD), 0)
    lane = lax.broadcasted_iota(jnp.int32, (rows_all, HD), 1)
    gather = (row // leaves * leaf_dev + row % leaf_dev == lane).astype(f32).astype(bf16)
    levels = jnp.dot(level, gather, preferred_element_type=f32).reshape(nodes, 8, HD)
    eye = identity(leaves)
    turned = [
        matmul_nt(eye, mean_t[:, g * leaves : (g + 1) * leaves]).reshape(nodes, leaf_dev, HD)
        for g in range(GROUP)
    ]
    out[...] = jnp.concatenate(turned + [levels], axis=1).astype(bf16)


def combine_kernel(parts, second, out):
    leaf_dev = out.shape[1] - SECOND
    span = GROUP * leaf_dev
    nodes = parts.shape[0]
    both = parts[...].astype(f32)
    mean = both[:, :span, :]
    lines = both[:, span:, :].reshape(nodes * 8, HD).astype(bf16)
    row = lax.broadcasted_iota(jnp.int32, (nodes * span, nodes * 8), 0)
    line = lax.broadcasted_iota(jnp.int32, (nodes * span, nodes * 8), 1)
    spread = ((row // span == line // 8) & (line % 8 < 3)).astype(f32).astype(bf16)
    level = jnp.dot(spread, lines, preferred_element_type=f32).reshape(nodes, span, HD)
    own = lax.broadcasted_iota(jnp.int32, level.shape, 2) == lax.broadcasted_iota(jnp.int32, level.shape, 1)
    level = jnp.sum(jnp.where(own, level, 0.0), axis=2, keepdims=True)
    top = jnp.max(level, axis=0, keepdims=True)
    weight = jnp.broadcast_to(jnp.exp2(level - top), mean.shape)
    result = jnp.sum(weight * mean, axis=0) / jnp.sum(weight, axis=0)
    mine = jnp.concatenate([result[g * leaf_dev : (g + 1) * leaf_dev] for g in range(GROUP)], axis=1)
    for index in range(out.shape[0]):
        rest = second[index].astype(f32)
        out[index] = jnp.concatenate([mine, rest[leaf_dev:]], axis=0).astype(bf16)


def output_kernel(attention, w_out_t, partial):
    nodes = attention.shape[0]
    leaf_dev = attention.shape[1] - SECOND
    rows = attention[:, :16, :].astype(f32)[:, :leaf_dev, :].reshape(nodes * leaf_dev, -1).astype(bf16)
    partial[...] = matmul_nt(rows, w_out_t[...]).astype(bf16)


def square_kernel(partial, projected, squares):
    total = jnp.sum(partial[...].astype(f32), axis=0)
    projected[...] = total
    sums = jnp.sum(total * total, axis=1, keepdims=True)
    leaves = total.shape[0]
    rows = lax.broadcasted_iota(jnp.int32, (leaves, HD), 0)
    cols = lax.broadcasted_iota(jnp.int32, (leaves, HD), 1)
    line = jnp.sum(jnp.where(rows == cols, sums, 0.0), axis=0, keepdims=True)
    squares[...] = jnp.broadcast_to(line, squares.shape)


def scale_kernel(squares, projected, gain, branch):
    leaves = projected.shape[0]
    line = jnp.sum(squares[...], axis=0, keepdims=True)
    rows = lax.broadcasted_iota(jnp.int32, (leaves, HD), 0)
    cols = lax.broadcasted_iota(jnp.int32, (leaves, HD), 1)
    sums = jnp.sum(jnp.where(rows == cols, line, 0.0), axis=1, keepdims=True)
    inverse = lax.rsqrt(sums / D + epsilon)
    branch[...] = (projected[...] * inverse * gain[...]).astype(bf16)


def children_kernel(matching, first, second, out):
    node = lax.axis_index("node")
    count = out.shape[0]
    leaf_dev = first.shape[1] - FIRST
    for index in range(count):
        place = node * count + index
        home = matching[place // HD, place % HD] // leaf_dev
        block = [first[home].astype(f32)[leaf_dev:], second[home].astype(f32)[leaf_dev:]]
        out[index] = jnp.concatenate(block, axis=0).astype(bf16)


def shards(
    states,
    w_query,
    w_key_value,
    w_out,
    post_gain,
    cache,
    tails,
    lengths,
    ancestry,
    block_node,
    matching,
):
    nodes = lax.axis_size("node")
    heads = lax.axis_size("head")
    leaves = states.shape[0]
    leaf_dev = leaves // nodes
    query_cols = w_query.shape[1]
    all_cols = 2 * query_cols + 3 * HD
    columns = w_out.shape[1]
    rows_all = leaves * GROUP
    child_dev = matching.shape[0] // nodes
    shape = jax.ShapeDtypeStruct

    cache_rows = cache.reshape(-1, 2 * HD)
    tail_rows = tails.reshape(-1, 2 * HD)
    key_count = cache_rows.shape[0]
    extended = key_count + leaf_dev * BLK
    matching_lines = matching.reshape(-1, HD)
    length_line = lengths.reshape(1, -1)

    partial, picks = call(
        project_kernel,
        (shape((leaves, all_cols), bf16), shape(matching_lines.shape, jnp.int32)),
        [HBM] * 4,
        (VMEM, VMEM),
        [
            pltpu.VMEM((states.shape[1], leaves), bf16),
            pltpu.VMEM(w_query.shape, bf16),
            pltpu.VMEM(w_key_value.shape, bf16),
            pltpu.VMEM(matching_lines.shape, jnp.int32),
            pltpu.SemaphoreType.DMA((4,)),
        ],
        vmem=60,
        cost=(2 * leaves * all_cols * states.shape[1], 1000000, 0),
    )(states.T, w_query, w_key_value, matching_lines)
    parts = lax.all_to_all(partial.reshape(nodes, leaf_dev, all_cols), "node", 0, 0, tiled=True)

    parts = parts.reshape(leaves, all_cols)
    sends, updated, second = call(
        home_kernel,
        (
            shape((nodes, leaf_dev + FIRST, 2 * HD), bf16),
            shape((leaf_dev * BLK, 2 * HD), bf16),
            shape((nodes, leaf_dev + SECOND, 2 * HD), bf16),
        ),
        [HBM] * 4,
        (VMEM, VMEM, VMEM),
        [
            pltpu.VMEM(parts.shape, bf16),
            pltpu.VMEM(tail_rows.shape, bf16),
            pltpu.VMEM(length_line.shape, jnp.int32),
            pltpu.VMEM((leaf_dev * BLK, 2 * HD), f32),
            pltpu.SMEM(matching_lines.shape, jnp.int32),
            pltpu.SemaphoreType.DMA((4,)),
        ],
        vmem=60,
        cost=(leaves * all_cols, 4 * leaves * all_cols, 0),
    )(parts, tail_rows, length_line, picks)
    rows = lax.all_to_all(sends, "node", 0, 0, tiled=True)

    span = GROUP * leaf_dev + 8
    sent = call(
        attend_kernel,
        shape((nodes, span, HD), bf16),
        [HBM] * 6,
        VMEM,
        [
            pltpu.VMEM((extended, rows_all), f32),
            pltpu.VMEM((VROWS, extended), bf16),
            pltpu.VMEM((leaf_dev * BLK, 2 * HD), bf16),
            pltpu.VMEM((block_node.shape[0], rows_all), f32),
            pltpu.VMEM(cache_rows.shape, bf16),
            pltpu.VMEM((nodes, 16, 2 * HD), bf16),
            pltpu.VMEM(ancestry.shape, jnp.int32),
            pltpu.VMEM((1, block_node.shape[0]), jnp.int32),
            pltpu.VMEM((1, leaf_dev), jnp.int32),
            pltpu.SemaphoreType.DMA((5 + key_count // CHUNK,)),
        ],
        vmem=60,
        cost=(4 * rows_all * extended * HD, 8 * HD * key_count, rows_all * extended),
    )(rows, cache_rows, updated, ancestry, block_node.reshape(1, -1), length_line)
    landed = lax.all_to_all(sent, "node", 0, 0, tiled=True)
    mine = call(
        combine_kernel,
        shape(second.shape, bf16),
        [VMEM, VMEM],
        VMEM,
        cost=(10 * rows_all * HD, 4 * rows_all * HD, rows_all * HD),
    )(landed, second)
    attention = lax.all_to_all(mine, "node", 0, 0, tiled=True)
    leaf_out = leaves // heads
    partial_out = call(
        output_kernel,
        shape((leaves, columns), bf16),
        [VMEM, VMEM],
        VMEM,
        cost=(2 * leaves * columns * query_cols, 6 * columns * query_cols, 0),
    )(attention, w_out.T)
    partial_out = lax.all_to_all(
        partial_out.reshape(heads, leaf_out, columns), "head", 0, 0, tiled=True
    )
    projected, squares = call(
        square_kernel,
        (shape((leaf_out, columns), f32), shape((nodes, HD), f32)),
        [VMEM],
        (VMEM, VMEM),
        cost=(leaves * columns, 4 * leaves * columns, 0),
    )(partial_out)
    squares = lax.all_to_all(squares.reshape(nodes, 1, HD), "node", 0, 0, tiled=True)
    children = call(
        children_kernel,
        shape((child_dev, BLK, 2 * HD), bf16),
        [SMEM, VMEM, VMEM],
        VMEM,
        cost=(1000000, 8 * child_dev * BLK * 2 * HD, 0),
    )(matching_lines, rows, attention)
    squares, children = lax.optimization_barrier((squares, children))
    branch = call(
        scale_kernel,
        shape((leaf_out, columns), bf16),
        [VMEM] * 3,
        VMEM,
    )(squares.reshape(nodes, HD), projected, post_gain.reshape(1, columns))
    return (branch, children.reshape(child_dev, BLK, 1, 2 * HD))


def solution(mesh):
    return jax.shard_map(
        shards,
        mesh=mesh,
        in_specs=(
            P(None, "node"),
            P("node", "head"),
            P("node", "head"),
            P("head", "node"),
            P("node"),
            P("node", None, "head", None),
            P("node", None, "head", None),
            P("node"),
            P(),
            P("node"),
            P(),
        ),
        out_specs=(P("head", "node"), P("node", None, "head", None)),
        check_vma=False,
    )
```

```python
import math

import jax
import jax.numpy as jnp
from jax import lax
from jax.experimental import pallas as pl
from jax.experimental.pallas import tpu as pltpu
from jax.sharding import PartitionSpec as P

D = 5376
HEADS = 32
KVH = 16
HD = 128
BLK = 64
GROUP = HEADS // KVH

score_scale = 168.0 ** (-0.5)
log2_scale = score_scale * math.log2(math.e)
neg_big = -1e30
epsilon = 1e-06
f32 = jnp.float32
bf16 = jnp.bfloat16
CHUNK = 3072
VROWS = HD + 16

VMEM = pl.BlockSpec(memory_space=pltpu.VMEM)
SMEM = pl.BlockSpec(memory_space=pltpu.SMEM)
HBM = pl.BlockSpec(memory_space=pltpu.HBM)


def call(kernel, out_shape, in_specs, out_specs, scratch=(), vmem=8, cost=(0, 0, 0)):
    return pl.pallas_call(
        kernel,
        out_shape=out_shape,
        in_specs=in_specs,
        out_specs=out_specs,
        scratch_shapes=list(scratch),
        compiler_params=pltpu.CompilerParams(vmem_limit_bytes=vmem * 1024 * 1024),
        cost_estimate=pl.CostEstimate(flops=cost[0], bytes_accessed=cost[1], transcendentals=cost[2]),
    )


def matmul_nt(a, b):
    return lax.dot_general(a, b, (((1,), (1,)), ((), ())), preferred_element_type=f32)


def identity(size):
    rows = lax.broadcasted_iota(jnp.int32, (size, size), 0)
    cols = lax.broadcasted_iota(jnp.int32, (size, size), 1)
    return (rows == cols).astype(f32).astype(bf16)


def halves(value):
    high = value.astype(bf16)
    return high, (value - high.astype(f32)).astype(bf16)


def project_kernel(
    states_hbm, query_hbm, key_value_hbm, matching_hbm, out, picks, states_t, w_query, w_key_value, matching, sems
):
    pairs = (
        (states_hbm, states_t),
        (query_hbm, w_query),
        (key_value_hbm, w_key_value),
        (matching_hbm, matching),
    )
    copies = [pltpu.make_async_copy(pair[0], pair[1], sems.at[i]) for i, pair in enumerate(pairs)]
    for copy in copies:
        copy.start()
    dims = (((0,), (0,)), ((), ()))
    cols = w_query.shape[1]
    copies[0].wait()
    copies[1].wait()
    query = lax.dot_general(states_t[...], w_query[...], dims, preferred_element_type=f32)
    out[:, :cols], out[:, cols : 2 * cols] = halves(query)
    copies[2].wait()
    fresh = lax.dot_general(states_t[...], w_key_value[...], dims, preferred_element_type=f32)
    out[:, 2 * cols :] = fresh.astype(bf16)
    copies[3].wait()
    node = lax.axis_index("node")
    child_dev = matching.shape[0] * HD // lax.axis_size("node")
    leaf_dev = states_t.shape[1] // lax.axis_size("node")
    parent = matching[...]
    first = node * leaf_dev
    own = (parent >= first) & (parent < first + leaf_dev)
    part = jnp.where(own, parent - first, 0).astype(f32).astype(bf16)
    of = lax.broadcasted_iota(jnp.int32, (HD, HD), 0) // child_dev
    to = lax.broadcasted_iota(jnp.int32, (HD, HD), 1) // child_dev
    same = (of == to).astype(f32).astype(bf16)
    picks[...] = jnp.dot(part, same, preferred_element_type=f32).astype(jnp.int32)


def home_kernel(parts, query_rep, fresh):
    leaf_dev = fresh.shape[0]
    total = jnp.sum(parts[...].astype(f32).reshape(-1, leaf_dev, parts.shape[1]), axis=0)
    cols = GROUP * HD
    query = total[:, :cols] + total[:, cols : 2 * cols]
    pair = jnp.concatenate([query, query], axis=0).astype(bf16)
    for index in range(query_rep.shape[0] // 16):
        query_rep[pl.ds(index * 16, 16), :] = pair
    fresh[...] = total[:, 2 * cols :]


def leaf_lengths(lengths):
    lanes = lax.broadcasted_iota(jnp.int32, lengths.shape, 1)
    return [
        jnp.sum(jnp.where(lanes == leaf, lengths[...], 0).astype(f32), axis=1, keepdims=True)
        for leaf in range(lengths.shape[1])
    ]


def attend_kernel(
    rows_hbm,
    cache_hbm,
    tails_hbm,
    fresh_hbm,
    ancestry_hbm,
    block_node_hbm,
    lengths_hbm,
    picks_hbm,
    out,
    scores,
    values_t,
    updated,
    bias,
    cache,
    queries,
    tails,
    fresh,
    ancestry,
    block_node,
    lengths,
    picks,
    sems,
):
    node = lax.axis_index("node")
    nodes = out.shape[0]
    leaf_dev = lengths.shape[1]
    leaves = queries.shape[0]
    cached = cache.shape[0]
    steps = range(0, cached, CHUNK)
    pairs = [
        (ancestry_hbm, ancestry),
        (block_node_hbm, block_node),
        (lengths_hbm, lengths),
        (tails_hbm, tails),
        (fresh_hbm, fresh),
        (picks_hbm, picks),
        (rows_hbm, queries),
    ]
    pairs += [(cache_hbm.at[pl.ds(start, CHUNK), :], cache.at[pl.ds(start, CHUNK), :]) for start in steps]
    copies = [pltpu.make_async_copy(pair[0], pair[1], sems.at[i]) for i, pair in enumerate(pairs)]
    for copy in copies:
        copy.start()
    for copy in copies[:2]:
        copy.wait()
    nodes_all = ancestry.shape[1]
    tree = lax.broadcasted_iota(jnp.int32, (nodes_all, block_node.shape[1]), 0)
    one_hot = (tree == block_node[...]).astype(f32).astype(bf16)
    seen = lax.dot_general(
        one_hot,
        ancestry[...].astype(f32).astype(bf16),
        (((0,), (1,)), ((), ())),
        preferred_element_type=f32,
    )
    shut = jnp.where(seen > 0.5, 0.0, neg_big)
    for g in range(GROUP):
        bias[:, g * leaves : (g + 1) * leaves] = shut
    eye = identity(HD)
    values_t[HD:, :] = jnp.ones((VROWS - HD, values_t.shape[1]), bf16)
    for copy in copies[2:6]:
        copy.wait()
    length = leaf_lengths(lengths)
    rows = lax.broadcasted_iota(jnp.int32, (BLK, 2 * HD), 0).astype(f32)
    for leaf in range(leaf_dev):
        span = pl.ds(leaf * BLK, BLK)
        block = jnp.where(rows < length[leaf], tails[span, :].astype(f32), 0.0)
        block = jnp.where(rows == length[leaf], fresh[leaf : leaf + 1, :], block)
        updated[span, :] = block.astype(bf16)
    values_t[:HD, cached:] = matmul_nt(eye, updated[:, HD:]).astype(bf16)
    rows_all = leaves * GROUP
    copies[6].wait()
    query = jnp.concatenate([queries[:, HD * g : HD * (g + 1)] for g in range(GROUP)], axis=0)
    own = updated.shape[0]
    top = jnp.full((8, rows_all), neg_big, f32)
    lanes = lax.broadcasted_iota(jnp.int32, (BLK, rows_all), 1) % leaves
    rows = lax.broadcasted_iota(jnp.int32, (BLK, rows_all), 0).astype(f32)
    raw = matmul_nt(updated[:, :HD], query)
    for leaf in range(leaf_dev):
        keep = (lanes == node * leaf_dev + leaf) & (rows <= length[leaf])
        part = jnp.where(keep, raw[leaf * BLK : (leaf + 1) * BLK] * log2_scale, neg_big)
        scores[pl.ds(cached + leaf * BLK, BLK), :] = part
        top = jnp.maximum(top, jnp.max(part.reshape(BLK // 8, 8, rows_all), axis=0))
    for step, start in enumerate(steps):
        copies[7 + step].wait()
        values_t[:HD, start : start + CHUNK] = matmul_nt(eye, cache[start : start + CHUNK, HD:]).astype(bf16)
        raw = matmul_nt(cache[start : start + CHUNK, :HD], query)
        for block in range(CHUNK // BLK):
            at = start // BLK + block
            part = raw[block * BLK : (block + 1) * BLK] * log2_scale + bias[at : at + 1, :]
            scores[pl.ds(start + block * BLK, BLK), :] = part
            top = jnp.maximum(top, jnp.max(part.reshape(BLK // 8, 8, rows_all), axis=0))
    row_max = jnp.max(top, axis=0, keepdims=True)
    total = jnp.zeros((VROWS, rows_all), f32)
    for start in range(0, cached + own, CHUNK):
        stop = min(start + CHUNK, cached + own)
        weights = jnp.exp2(scores[start:stop, :] - row_max).astype(bf16)
        total = total + jnp.dot(values_t[:, start:stop], weights, preferred_element_type=f32)
    weight_sum = total[HD : HD + 1]
    mean_t = (total[:HD] / weight_sum).astype(bf16)
    level = row_max + jnp.log2(weight_sum)
    high = level.astype(bf16).astype(f32)
    middle = (level - high).astype(bf16).astype(f32)
    low = level - high - middle
    lines = (nodes * 8, rows_all)
    line = lax.broadcasted_iota(jnp.int32, lines, 0)
    row = lax.broadcasted_iota(jnp.int32, lines, 1)
    part = line % 8
    level = jnp.where(part == 0, high, jnp.where(part == 1, middle, jnp.where(part == 2, low, 0.0)))
    level = jnp.where(row % leaves // leaf_dev == line // 8, level, 0.0).astype(bf16)
    row = lax.broadcasted_iota(jnp.int32, (rows_all, HD), 0)
    lane = lax.broadcasted_iota(jnp.int32, (rows_all, HD), 1)
    gather = (row // leaves * leaf_dev + row % leaf_dev == lane).astype(f32).astype(bf16)
    levels = jnp.dot(level, gather, preferred_element_type=f32)
    line = lax.broadcasted_iota(jnp.int32, (nodes * 8, picks.shape[0]), 0)
    spot = lax.broadcasted_iota(jnp.int32, (nodes * 8, picks.shape[0]), 1)
    per_line = nodes // picks.shape[0]
    lift = (line // (8 * per_line) == spot).astype(f32).astype(bf16)
    pick = jnp.dot(lift, picks[...].astype(f32).astype(bf16), preferred_element_type=f32)
    line = lax.broadcasted_iota(jnp.int32, pick.shape, 0)
    lane = lax.broadcasted_iota(jnp.int32, pick.shape, 1)
    chosen = lane == line // 8 % per_line * (HD // per_line)
    pick = jnp.sum(jnp.where(chosen, pick, 0.0), axis=1, keepdims=True)
    line = lax.broadcasted_iota(jnp.int32, (nodes * 8, 3 * leaf_dev), 0)
    of = lax.broadcasted_iota(jnp.int32, (nodes * 8, 3 * leaf_dev), 1)
    hit = (of % leaf_dev == pick.astype(jnp.int32)) & (of // leaf_dev == line % 8 - 3)
    sizes = jnp.concatenate([jnp.broadcast_to(value, (1, HD)) for value in length], axis=0)
    source = jnp.concatenate([sizes, fresh[:, :HD], fresh[:, HD:]], axis=0).astype(bf16)
    levels = levels + jnp.dot(hit.astype(f32).astype(bf16), source, preferred_element_type=f32)
    levels = levels.reshape(nodes, 8, HD)
    eye = identity(leaves)
    turned = [
        matmul_nt(eye, mean_t[:, g * leaves : (g + 1) * leaves]).reshape(nodes, leaf_dev, HD)
        for g in range(GROUP)
    ]
    out[...] = jnp.concatenate(turned + [levels], axis=1).astype(bf16)


def combine_kernel(parts, out):
    nodes = parts.shape[0]
    leaf_dev = out.shape[0] // nodes
    span = GROUP * leaf_dev
    both = parts[...].astype(f32)
    mean = both[:, :span, :]
    lines = both[:, span:, :].reshape(nodes * 8, HD).astype(bf16)
    row = lax.broadcasted_iota(jnp.int32, (nodes * span, nodes * 8), 0)
    line = lax.broadcasted_iota(jnp.int32, (nodes * span, nodes * 8), 1)
    spread = ((row // span == line // 8) & (line % 8 < 3)).astype(f32).astype(bf16)
    level = jnp.dot(spread, lines, preferred_element_type=f32).reshape(nodes, span, HD)
    own = lax.broadcasted_iota(jnp.int32, level.shape, 2) == lax.broadcasted_iota(jnp.int32, level.shape, 1)
    level = jnp.sum(jnp.where(own, level, 0.0), axis=2, keepdims=True)
    top = jnp.max(level, axis=0, keepdims=True)
    weight = jnp.broadcast_to(jnp.exp2(level - top), mean.shape)
    result = jnp.sum(weight * mean, axis=0) / jnp.sum(weight, axis=0)
    mine = jnp.concatenate([result[g * leaf_dev : (g + 1) * leaf_dev] for g in range(GROUP)], axis=1)
    pair = jnp.concatenate([mine, mine], axis=0).astype(bf16)
    for index in range(out.shape[0] // 16):
        out[pl.ds(index * 16, 16), :] = pair


def output_kernel(attention, w_out_t, partial):
    partial[...] = matmul_nt(attention[...], w_out_t[...]).astype(bf16)


def square_kernel(partial, projected, squares):
    total = jnp.sum(partial[...].astype(f32), axis=0)
    projected[...] = total
    sums = jnp.sum(total * total, axis=1, keepdims=True)
    leaves = total.shape[0]
    rows = lax.broadcasted_iota(jnp.int32, (leaves, HD), 0)
    cols = lax.broadcasted_iota(jnp.int32, (leaves, HD), 1)
    line = jnp.sum(jnp.where(rows == cols, sums, 0.0), axis=0, keepdims=True)
    squares[...] = jnp.broadcast_to(line, squares.shape)


def scale_kernel(squares, projected, gain, branch):
    leaves = projected.shape[0]
    line = jnp.sum(squares[...], axis=0, keepdims=True)
    rows = lax.broadcasted_iota(jnp.int32, (leaves, HD), 0)
    cols = lax.broadcasted_iota(jnp.int32, (leaves, HD), 1)
    sums = jnp.sum(jnp.where(rows == cols, line, 0.0), axis=1, keepdims=True)
    inverse = lax.rsqrt(sums / D + epsilon)
    branch[...] = (projected[...] * inverse * gain[...]).astype(bf16)


def children_kernel(
    matching_hbm, tails, landed_hbm, out, matching, landed, blocks, built, sems, in_sems, out_sems
):
    node = lax.axis_index("node")
    count = out.shape[0]
    leaf_dev = tails.shape[0] // landed.shape[0]
    table = pltpu.make_async_copy(matching_hbm, matching, sems.at[0])
    table.start()
    extra = pltpu.make_async_copy(landed_hbm, landed, sems.at[1])
    extra.start()
    table.wait()
    parents = []
    fetches = []
    for index in range(count):
        place = node * count + index
        parent = matching[place // HD, place % HD]
        copy = pltpu.make_async_copy(tails.at[parent], blocks.at[index], in_sems.at[index])
        copy.start()
        parents.append(parent)
        fetches.append(copy)
    extra.wait()
    rows = lax.broadcasted_iota(jnp.int32, (BLK, 2 * HD), 0).astype(f32)
    span = landed.shape[1] - 8
    stores = []
    for index in range(count):
        lines = landed[parents[index] // leaf_dev].astype(f32)[span:]
        length = lines[3:4, 0:1]
        fresh = jnp.concatenate([lines[4:5], lines[5:6]], axis=1)
        fetches[index].wait()
        block = jnp.where(rows < length, blocks[index].astype(f32), 0.0)
        built[index] = jnp.where(rows == length, fresh, block).astype(bf16)
        copy = pltpu.make_async_copy(built.at[index], out.at[index], out_sems.at[index])
        copy.start()
        stores.append(copy)
    for copy in stores:
        copy.wait()


def shards(
    states,
    w_query,
    w_key_value,
    w_out,
    post_gain,
    cache,
    tails,
    lengths,
    ancestry,
    block_node,
    matching,
):
    nodes = lax.axis_size("node")
    heads = lax.axis_size("head")
    leaves = states.shape[0]
    leaf_dev = leaves // nodes
    query_cols = w_query.shape[1]
    all_cols = 2 * query_cols + w_key_value.shape[1]
    columns = w_out.shape[1]
    rows_all = leaves * GROUP
    child_dev = matching.shape[0] // nodes
    shape = jax.ShapeDtypeStruct

    cache_rows = cache.reshape(-1, 2 * HD)
    tail_rows = tails.reshape(-1, 2 * HD)
    key_count = cache_rows.shape[0]
    extended = key_count + leaf_dev * BLK
    all_tails = lax.all_gather(tail_rows, "node", axis=0, tiled=True)
    matching_lines = matching.reshape(-1, HD)
    length_line = lengths.reshape(1, -1)

    partial, picks = call(
        project_kernel,
        (shape((leaves, all_cols), bf16), shape(matching_lines.shape, jnp.int32)),
        [HBM] * 4,
        (VMEM, VMEM),
        [
            pltpu.VMEM((states.shape[1], leaves), bf16),
            pltpu.VMEM(w_query.shape, bf16),
            pltpu.VMEM(w_key_value.shape, bf16),
            pltpu.VMEM(matching_lines.shape, jnp.int32),
            pltpu.SemaphoreType.DMA((4,)),
        ],
        vmem=60,
        cost=(2 * leaves * all_cols * states.shape[1], 1000000, 0),
    )(states.T, w_query, w_key_value, matching_lines)
    parts = lax.all_to_all(partial.reshape(nodes, leaf_dev, all_cols), "node", 0, 0, tiled=True)

    parts = parts.reshape(leaves, all_cols)
    query_rep, fresh = call(
        home_kernel,
        (shape((leaves, query_cols), bf16), shape((leaf_dev, 2 * HD), f32)),
        [VMEM],
        (VMEM, VMEM),
        cost=(leaves * all_cols, 4 * leaves * all_cols, 0),
    )(parts)
    rows = lax.all_to_all(query_rep.reshape(nodes, leaf_dev, query_cols), "node", 0, 0, tiled=True)

    span = GROUP * leaf_dev + 8
    sent = call(
        attend_kernel,
        shape((nodes, span, HD), bf16),
        [HBM] * 8,
        VMEM,
        [
            pltpu.VMEM((extended, rows_all), f32),
            pltpu.VMEM((VROWS, extended), bf16),
            pltpu.VMEM((leaf_dev * BLK, 2 * HD), bf16),
            pltpu.VMEM((block_node.shape[0], rows_all), f32),
            pltpu.VMEM(cache_rows.shape, bf16),
            pltpu.VMEM((leaves, query_cols), bf16),
            pltpu.VMEM(tail_rows.shape, bf16),
            pltpu.VMEM(fresh.shape, f32),
            pltpu.VMEM(ancestry.shape, jnp.int32),
            pltpu.VMEM((1, block_node.shape[0]), jnp.int32),
            pltpu.VMEM((1, leaf_dev), jnp.int32),
            pltpu.VMEM(picks.shape, jnp.int32),
            pltpu.SemaphoreType.DMA((7 + key_count // CHUNK,)),
        ],
        vmem=60,
        cost=(4 * rows_all * extended * HD, 8 * HD * key_count, rows_all * extended),
    )(
        rows.reshape(leaves, query_cols),
        cache_rows,
        tail_rows,
        fresh,
        ancestry,
        block_node.reshape(1, -1),
        length_line,
        picks,
    )
    landed = lax.all_to_all(sent, "node", 0, 0, tiled=True)
    mine = call(
        combine_kernel,
        shape((leaves, query_cols), bf16),
        [VMEM],
        VMEM,
        cost=(10 * rows_all * HD, 4 * rows_all * HD, rows_all * HD),
    )(landed)
    attention = lax.all_to_all(mine.reshape(nodes, leaf_dev, query_cols), "node", 0, 0, tiled=True)
    leaf_out = leaves // heads
    partial_out = call(
        output_kernel,
        shape((leaves, columns), bf16),
        [VMEM, VMEM],
        VMEM,
        cost=(2 * leaves * columns * query_cols, 6 * columns * query_cols, 0),
    )(attention.reshape(leaves, query_cols), w_out.T)
    partial_out = lax.all_to_all(
        partial_out.reshape(heads, leaf_out, columns), "head", 0, 0, tiled=True
    )
    projected, squares = call(
        square_kernel,
        (shape((leaf_out, columns), f32), shape((nodes, HD), f32)),
        [VMEM],
        (VMEM, VMEM),
        cost=(leaves * columns, 4 * leaves * columns, 0),
    )(partial_out)
    squares = lax.all_to_all(squares.reshape(nodes, 1, HD), "node", 0, 0, tiled=True)
    children = call(
        children_kernel,
        shape((child_dev, BLK, 2 * HD), bf16),
        [HBM] * 3,
        HBM,
        [
            pltpu.SMEM(matching_lines.shape, jnp.int32),
            pltpu.VMEM(landed.shape, bf16),
            pltpu.VMEM((child_dev, BLK, 2 * HD), bf16),
            pltpu.VMEM((child_dev, BLK, 2 * HD), bf16),
            pltpu.SemaphoreType.DMA((2,)),
            pltpu.SemaphoreType.DMA((child_dev,)),
            pltpu.SemaphoreType.DMA((child_dev,)),
        ],
        vmem=60,
        cost=(1000000, 8 * child_dev * BLK * 2 * HD, 0),
    )(matching_lines, all_tails.reshape(leaves, BLK, 2 * HD), landed)
    squares, children = lax.optimization_barrier((squares, children))
    branch = call(
        scale_kernel,
        shape((leaf_out, columns), bf16),
        [VMEM] * 3,
        VMEM,
    )(squares.reshape(nodes, HD), projected, post_gain.reshape(1, columns))
    return (branch, children.reshape(child_dev, BLK, 1, 2 * HD))


def solution(mesh):
    return jax.shard_map(
        shards,
        mesh=mesh,
        in_specs=(
            P(None, "node"),
            P("node", "head"),
            P("node", "head"),
            P("head", "node"),
            P("node"),
            P("node", None, "head", None),
            P("node", None, "head", None),
            P("node"),
            P(),
            P("node"),
            P(),
        ),
        out_specs=(P("head", "node"), P("node", None, "head", None)),
        check_vma=False,
    )
```

```python
import math

import jax
import jax.numpy as jnp
from jax import lax
from jax.experimental import pallas as pl
from jax.experimental.pallas import tpu as pltpu
from jax.sharding import PartitionSpec as P

D = 5376
HEADS = 32
KVH = 16
HD = 128
BLK = 64
GROUP = HEADS // KVH

score_scale = 168.0 ** (-0.5)
log2_scale = score_scale * math.log2(math.e)
neg_big = -1e30
epsilon = 1e-06
f32 = jnp.float32
bf16 = jnp.bfloat16
CHUNK = 3072
VROWS = HD + 16
GATHER = 8

VMEM = pl.BlockSpec(memory_space=pltpu.VMEM)
SMEM = pl.BlockSpec(memory_space=pltpu.SMEM)
HBM = pl.BlockSpec(memory_space=pltpu.HBM)


def call(kernel, out_shape, in_specs, out_specs, scratch=(), vmem=8, cost=(0, 0, 0)):
    return pl.pallas_call(
        kernel,
        out_shape=out_shape,
        in_specs=in_specs,
        out_specs=out_specs,
        scratch_shapes=list(scratch),
        compiler_params=pltpu.CompilerParams(vmem_limit_bytes=vmem * 1024 * 1024),
        cost_estimate=pl.CostEstimate(flops=cost[0], bytes_accessed=cost[1], transcendentals=cost[2]),
    )


def matmul_nt(a, b):
    return lax.dot_general(a, b, (((1,), (1,)), ((), ())), preferred_element_type=f32)


def identity(size):
    rows = lax.broadcasted_iota(jnp.int32, (size, size), 0)
    cols = lax.broadcasted_iota(jnp.int32, (size, size), 1)
    return (rows == cols).astype(f32).astype(bf16)


def halves(value):
    high = value.astype(bf16)
    return high, (value - high.astype(f32)).astype(bf16)


def project_kernel(
    states_hbm, query_hbm, key_value_hbm, matching_hbm, out, picks, states_t, w_query, w_key_value, matching, sems
):
    pairs = (
        (states_hbm, states_t),
        (query_hbm, w_query),
        (key_value_hbm, w_key_value),
        (matching_hbm, matching),
    )
    copies = [pltpu.make_async_copy(pair[0], pair[1], sems.at[i]) for i, pair in enumerate(pairs)]
    for copy in copies:
        copy.start()
    dims = (((0,), (0,)), ((), ()))
    cols = w_query.shape[1]
    for copy in copies:
        copy.wait()
    query = lax.dot_general(states_t[...], w_query[...], dims, preferred_element_type=f32)
    out[:, :cols], out[:, cols : 2 * cols] = halves(query)
    fresh = lax.dot_general(states_t[...], w_key_value[...], dims, preferred_element_type=f32)
    out[:, 2 * cols :] = fresh.astype(bf16)
    node = lax.axis_index("node")
    child_dev = matching.shape[0] * HD // lax.axis_size("node")
    leaf_dev = states_t.shape[1] // lax.axis_size("node")
    parent = matching[...]
    first = node * leaf_dev
    own = (parent >= first) & (parent < first + leaf_dev)
    part = jnp.where(own, parent - first, 0).astype(f32).astype(bf16)
    of = lax.broadcasted_iota(jnp.int32, (HD, HD), 0) // child_dev
    to = lax.broadcasted_iota(jnp.int32, (HD, HD), 1) // child_dev
    same = (of == to).astype(f32).astype(bf16)
    picks[...] = jnp.dot(part, same, preferred_element_type=f32).astype(jnp.int32)


def home_kernel(parts, query_rep, fresh):
    leaf_dev = fresh.shape[0]
    total = jnp.sum(parts[...].astype(f32).reshape(-1, leaf_dev, parts.shape[1]), axis=0)
    cols = GROUP * HD
    query = total[:, :cols] + total[:, cols : 2 * cols]
    pair = jnp.concatenate([query, query], axis=0).astype(bf16)
    for index in range(query_rep.shape[0] // 16):
        query_rep[pl.ds(index * 16, 16), :] = pair
    fresh[...] = total[:, 2 * cols :]


def leaf_lengths(lengths):
    lanes = lax.broadcasted_iota(jnp.int32, lengths.shape, 1)
    return [
        jnp.sum(jnp.where(lanes == leaf, lengths[...], 0).astype(f32), axis=1, keepdims=True)
        for leaf in range(lengths.shape[1])
    ]


def attend_kernel(
    rows_hbm,
    cache_hbm,
    tails_hbm,
    fresh_hbm,
    ancestry_hbm,
    block_node_hbm,
    lengths_hbm,
    picks_hbm,
    out,
    scores,
    values_t,
    updated,
    bias,
    cache,
    queries,
    tails,
    fresh,
    ancestry,
    block_node,
    lengths,
    picks,
    sems,
):
    node = lax.axis_index("node")
    nodes = out.shape[0]
    leaf_dev = lengths.shape[1]
    leaves = queries.shape[0]
    cached = cache.shape[0]
    steps = range(0, cached, CHUNK)
    pairs = [
        (ancestry_hbm, ancestry),
        (block_node_hbm, block_node),
        (lengths_hbm, lengths),
        (tails_hbm, tails),
        (fresh_hbm, fresh),
        (picks_hbm, picks),
        (rows_hbm, queries),
    ]
    pairs += [(cache_hbm.at[pl.ds(start, CHUNK), :], cache.at[pl.ds(start, CHUNK), :]) for start in steps]
    copies = [pltpu.make_async_copy(pair[0], pair[1], sems.at[i]) for i, pair in enumerate(pairs)]
    for copy in copies:
        copy.start()
    for copy in copies[:2]:
        copy.wait()
    nodes_all = ancestry.shape[1]
    tree = lax.broadcasted_iota(jnp.int32, (nodes_all, block_node.shape[1]), 0)
    one_hot = (tree == block_node[...]).astype(f32).astype(bf16)
    seen = lax.dot_general(
        one_hot,
        ancestry[...].astype(f32).astype(bf16),
        (((0,), (1,)), ((), ())),
        preferred_element_type=f32,
    )
    shut = jnp.where(seen > 0.5, 0.0, neg_big)
    for g in range(GROUP):
        bias[:, g * leaves : (g + 1) * leaves] = shut
    eye = identity(HD)
    values_t[HD:, :] = jnp.ones((VROWS - HD, values_t.shape[1]), bf16)
    for copy in copies[2:6]:
        copy.wait()
    length = leaf_lengths(lengths)
    rows = lax.broadcasted_iota(jnp.int32, (BLK, 2 * HD), 0).astype(f32)
    for leaf in range(leaf_dev):
        span = pl.ds(leaf * BLK, BLK)
        block = jnp.where(rows < length[leaf], tails[span, :].astype(f32), 0.0)
        block = jnp.where(rows == length[leaf], fresh[leaf : leaf + 1, :], block)
        updated[span, :] = block.astype(bf16)
    values_t[:HD, cached:] = matmul_nt(eye, updated[:, HD:]).astype(bf16)
    rows_all = leaves * GROUP
    copies[6].wait()
    query = jnp.concatenate([queries[:, HD * g : HD * (g + 1)] for g in range(GROUP)], axis=0)
    own = updated.shape[0]
    top = jnp.full((8, rows_all), neg_big, f32)
    lanes = lax.broadcasted_iota(jnp.int32, (BLK, rows_all), 1) % leaves
    rows = lax.broadcasted_iota(jnp.int32, (BLK, rows_all), 0).astype(f32)
    raw = matmul_nt(updated[:, :HD], query)
    for leaf in range(leaf_dev):
        keep = (lanes == node * leaf_dev + leaf) & (rows <= length[leaf])
        part = jnp.where(keep, raw[leaf * BLK : (leaf + 1) * BLK] * log2_scale, neg_big)
        scores[pl.ds(cached + leaf * BLK, BLK), :] = part
        top = jnp.maximum(top, jnp.max(part.reshape(BLK // 8, 8, rows_all), axis=0))
    for step, start in enumerate(steps):
        copies[7 + step].wait()
        values_t[:HD, start : start + CHUNK] = matmul_nt(eye, cache[start : start + CHUNK, HD:]).astype(bf16)
        raw = matmul_nt(cache[start : start + CHUNK, :HD], query)
        for block in range(CHUNK // BLK):
            at = start // BLK + block
            part = raw[block * BLK : (block + 1) * BLK] * log2_scale + bias[at : at + 1, :]
            scores[pl.ds(start + block * BLK, BLK), :] = part
            top = jnp.maximum(top, jnp.max(part.reshape(BLK // 8, 8, rows_all), axis=0))
    row_max = jnp.max(top, axis=0, keepdims=True)
    total = jnp.zeros((VROWS, rows_all), f32)
    for start in range(0, cached + own, CHUNK):
        stop = min(start + CHUNK, cached + own)
        weights = jnp.exp2(scores[start:stop, :] - row_max).astype(bf16)
        total = total + jnp.dot(values_t[:, start:stop], weights, preferred_element_type=f32)
    weight_sum = total[HD : HD + 1]
    mean_t = (total[:HD] / weight_sum).astype(bf16)
    level = row_max + jnp.log2(weight_sum)
    high = level.astype(bf16).astype(f32)
    middle = (level - high).astype(bf16).astype(f32)
    low = level - high - middle
    lines = (nodes * 8, rows_all)
    line = lax.broadcasted_iota(jnp.int32, lines, 0)
    row = lax.broadcasted_iota(jnp.int32, lines, 1)
    part = line % 8
    level = jnp.where(part == 0, high, jnp.where(part == 1, middle, jnp.where(part == 2, low, 0.0)))
    level = jnp.where(row % leaves // leaf_dev == line // 8, level, 0.0).astype(bf16)
    row = lax.broadcasted_iota(jnp.int32, (rows_all, HD), 0)
    lane = lax.broadcasted_iota(jnp.int32, (rows_all, HD), 1)
    gather = (row // leaves * leaf_dev + row % leaf_dev == lane).astype(f32).astype(bf16)
    levels = jnp.dot(level, gather, preferred_element_type=f32)
    line = lax.broadcasted_iota(jnp.int32, (nodes * 8, picks.shape[0]), 0)
    spot = lax.broadcasted_iota(jnp.int32, (nodes * 8, picks.shape[0]), 1)
    per_line = nodes // picks.shape[0]
    lift = (line // (8 * per_line) == spot).astype(f32).astype(bf16)
    pick = jnp.dot(lift, picks[...].astype(f32).astype(bf16), preferred_element_type=f32)
    line = lax.broadcasted_iota(jnp.int32, pick.shape, 0)
    lane = lax.broadcasted_iota(jnp.int32, pick.shape, 1)
    chosen = lane == line // 8 % per_line * (HD // per_line)
    pick = jnp.sum(jnp.where(chosen, pick, 0.0), axis=1, keepdims=True)
    line = lax.broadcasted_iota(jnp.int32, (nodes * 8, 3 * leaf_dev), 0)
    of = lax.broadcasted_iota(jnp.int32, (nodes * 8, 3 * leaf_dev), 1)
    hit = (of % leaf_dev == pick.astype(jnp.int32)) & (of // leaf_dev == line % 8 - 3)
    sizes = jnp.concatenate([jnp.broadcast_to(value, (1, HD)) for value in length], axis=0)
    source = jnp.concatenate([sizes, fresh[:, :HD], fresh[:, HD:]], axis=0).astype(bf16)
    levels = levels + jnp.dot(hit.astype(f32).astype(bf16), source, preferred_element_type=f32)
    levels = levels.reshape(nodes, 8, HD)
    eye = identity(leaves)
    turned = [
        matmul_nt(eye, mean_t[:, g * leaves : (g + 1) * leaves]).reshape(nodes, leaf_dev, HD)
        for g in range(GROUP)
    ]
    out[...] = jnp.concatenate(turned + [levels], axis=1).astype(bf16)


def combine_kernel(parts, out):
    nodes = parts.shape[0]
    leaf_dev = out.shape[0] // nodes
    span = GROUP * leaf_dev
    both = parts[...].astype(f32)
    mean = both[:, :span, :]
    lines = both[:, span:, :].reshape(nodes * 8, HD).astype(bf16)
    row = lax.broadcasted_iota(jnp.int32, (nodes * span, nodes * 8), 0)
    line = lax.broadcasted_iota(jnp.int32, (nodes * span, nodes * 8), 1)
    spread = ((row // span == line // 8) & (line % 8 < 3)).astype(f32).astype(bf16)
    level = jnp.dot(spread, lines, preferred_element_type=f32).reshape(nodes, span, HD)
    own = lax.broadcasted_iota(jnp.int32, level.shape, 2) == lax.broadcasted_iota(jnp.int32, level.shape, 1)
    level = jnp.sum(jnp.where(own, level, 0.0), axis=2, keepdims=True)
    top = jnp.max(level, axis=0, keepdims=True)
    weight = jnp.broadcast_to(jnp.exp2(level - top), mean.shape)
    result = jnp.sum(weight * mean, axis=0) / jnp.sum(weight, axis=0)
    mine = jnp.concatenate([result[g * leaf_dev : (g + 1) * leaf_dev] for g in range(GROUP)], axis=1)
    pair = jnp.concatenate([mine, mine], axis=0).astype(bf16)
    for index in range(out.shape[0] // 16):
        out[pl.ds(index * 16, 16), :] = pair


def output_kernel(attention, w_out_t, partial):
    partial[...] = matmul_nt(attention[...], w_out_t[...]).astype(bf16)


def square_kernel(partial, projected, squares):
    total = jnp.sum(partial[...].astype(f32), axis=0)
    projected[...] = total
    sums = jnp.sum(total * total, axis=1, keepdims=True)
    leaves = total.shape[0]
    rows = lax.broadcasted_iota(jnp.int32, (leaves, HD), 0)
    cols = lax.broadcasted_iota(jnp.int32, (leaves, HD), 1)
    line = jnp.sum(jnp.where(rows == cols, sums, 0.0), axis=0, keepdims=True)
    squares[...] = jnp.broadcast_to(line, squares.shape)


def scale_kernel(squares, projected, gain, branch):
    leaves = projected.shape[0]
    line = jnp.sum(squares[...], axis=0, keepdims=True)
    rows = lax.broadcasted_iota(jnp.int32, (leaves, HD), 0)
    cols = lax.broadcasted_iota(jnp.int32, (leaves, HD), 1)
    sums = jnp.sum(jnp.where(rows == cols, line, 0.0), axis=1, keepdims=True)
    inverse = lax.rsqrt(sums / D + epsilon)
    branch[...] = (projected[...] * inverse * gain[...]).astype(bf16)


def children_kernel(
    matching_hbm, tails, landed_hbm, out, matching, landed, blocks, built, sems, in_sems, out_sems
):
    node = lax.axis_index("node")
    count = out.shape[0]
    leaf_dev = tails.shape[0] // landed.shape[0]
    table = pltpu.make_async_copy(matching_hbm, matching, sems.at[0])
    table.start()
    extra = pltpu.make_async_copy(landed_hbm, landed, sems.at[1])
    extra.start()
    table.wait()
    parents = []
    fetches = []
    for index in range(count):
        place = node * count + index
        parent = matching[place // HD, place % HD]
        copy = pltpu.make_async_copy(tails.at[parent], blocks.at[index], in_sems.at[index])
        copy.start()
        parents.append(parent)
        fetches.append(copy)
    extra.wait()
    rows = lax.broadcasted_iota(jnp.int32, (BLK, 2 * HD), 0).astype(f32)
    span = landed.shape[1] - 8
    lengths = []
    fresh = []
    for parent in parents:
        lines = landed[parent // leaf_dev].astype(f32)[span:]
        lengths.append(jnp.broadcast_to(lines[3:4, 0:1], (1, 2 * HD)))
        fresh.append(jnp.concatenate([lines[4:5], lines[5:6]], axis=1))
    stores = []
    for first in range(0, count, GATHER):
        group = range(first, first + GATHER)
        for index in group:
            fetches[index].wait()
        for index in group:
            block = jnp.where(rows < lengths[index], blocks[index].astype(f32), 0.0)
            built[index] = jnp.where(rows == lengths[index], fresh[index], block).astype(bf16)
        copy = pltpu.make_async_copy(
            built.at[pl.ds(first, GATHER)], out.at[pl.ds(first, GATHER)], out_sems.at[first // GATHER]
        )
        copy.start()
        stores.append(copy)
    for copy in stores:
        copy.wait()


def shards(
    states,
    w_query,
    w_key_value,
    w_out,
    post_gain,
    cache,
    tails,
    lengths,
    ancestry,
    block_node,
    matching,
):
    nodes = lax.axis_size("node")
    heads = lax.axis_size("head")
    leaves = states.shape[0]
    leaf_dev = leaves // nodes
    query_cols = w_query.shape[1]
    all_cols = 2 * query_cols + w_key_value.shape[1]
    columns = w_out.shape[1]
    rows_all = leaves * GROUP
    child_dev = matching.shape[0] // nodes
    shape = jax.ShapeDtypeStruct

    cache_rows = cache.reshape(-1, 2 * HD)
    tail_rows = tails.reshape(-1, 2 * HD)
    key_count = cache_rows.shape[0]
    extended = key_count + leaf_dev * BLK
    all_tails = lax.all_gather(tail_rows, "node", axis=0, tiled=True)
    matching_lines = matching.reshape(-1, HD)
    length_line = lengths.reshape(1, -1)

    partial, picks = call(
        project_kernel,
        (shape((leaves, all_cols), bf16), shape(matching_lines.shape, jnp.int32)),
        [HBM] * 4,
        (VMEM, VMEM),
        [
            pltpu.VMEM((states.shape[1], leaves), bf16),
            pltpu.VMEM(w_query.shape, bf16),
            pltpu.VMEM(w_key_value.shape, bf16),
            pltpu.VMEM(matching_lines.shape, jnp.int32),
            pltpu.SemaphoreType.DMA((4,)),
        ],
        vmem=60,
        cost=(2 * leaves * all_cols * states.shape[1], 1000000, 0),
    )(states.T, w_query, w_key_value, matching_lines)
    parts = lax.all_to_all(partial.reshape(nodes, leaf_dev, all_cols), "node", 0, 0, tiled=True)

    parts = parts.reshape(leaves, all_cols)
    query_rep, fresh = call(
        home_kernel,
        (shape((leaves, query_cols), bf16), shape((leaf_dev, 2 * HD), f32)),
        [VMEM],
        (VMEM, VMEM),
        cost=(leaves * all_cols, 4 * leaves * all_cols, 0),
    )(parts)
    rows = lax.all_to_all(query_rep.reshape(nodes, leaf_dev, query_cols), "node", 0, 0, tiled=True)

    span = GROUP * leaf_dev + 8
    sent = call(
        attend_kernel,
        shape((nodes, span, HD), bf16),
        [HBM] * 8,
        VMEM,
        [
            pltpu.VMEM((extended, rows_all), f32),
            pltpu.VMEM((VROWS, extended), bf16),
            pltpu.VMEM((leaf_dev * BLK, 2 * HD), bf16),
            pltpu.VMEM((block_node.shape[0], rows_all), f32),
            pltpu.VMEM(cache_rows.shape, bf16),
            pltpu.VMEM((leaves, query_cols), bf16),
            pltpu.VMEM(tail_rows.shape, bf16),
            pltpu.VMEM(fresh.shape, f32),
            pltpu.VMEM(ancestry.shape, jnp.int32),
            pltpu.VMEM((1, block_node.shape[0]), jnp.int32),
            pltpu.VMEM((1, leaf_dev), jnp.int32),
            pltpu.VMEM(picks.shape, jnp.int32),
            pltpu.SemaphoreType.DMA((7 + key_count // CHUNK,)),
        ],
        vmem=60,
        cost=(4 * rows_all * extended * HD, 8 * HD * key_count, rows_all * extended),
    )(
        rows.reshape(leaves, query_cols),
        cache_rows,
        tail_rows,
        fresh,
        ancestry,
        block_node.reshape(1, -1),
        length_line,
        picks,
    )
    landed = lax.all_to_all(sent, "node", 0, 0, tiled=True)
    mine = call(
        combine_kernel,
        shape((leaves, query_cols), bf16),
        [VMEM],
        VMEM,
        cost=(10 * rows_all * HD, 4 * rows_all * HD, rows_all * HD),
    )(landed)
    attention = lax.all_to_all(mine.reshape(nodes, leaf_dev, query_cols), "node", 0, 0, tiled=True)
    leaf_out = leaves // heads
    partial_out = call(
        output_kernel,
        shape((leaves, columns), bf16),
        [VMEM, VMEM],
        VMEM,
        cost=(2 * leaves * columns * query_cols, 6 * columns * query_cols, 0),
    )(attention.reshape(leaves, query_cols), w_out.T)
    partial_out = lax.all_to_all(
        partial_out.reshape(heads, leaf_out, columns), "head", 0, 0, tiled=True
    )
    projected, squares = call(
        square_kernel,
        (shape((leaf_out, columns), f32), shape((nodes, HD), f32)),
        [VMEM],
        (VMEM, VMEM),
        cost=(leaves * columns, 4 * leaves * columns, 0),
    )(partial_out)
    squares = lax.all_to_all(squares.reshape(nodes, 1, HD), "node", 0, 0, tiled=True)
    children = call(
        children_kernel,
        shape((child_dev, BLK, 2 * HD), bf16),
        [HBM] * 3,
        HBM,
        [
            pltpu.SMEM(matching_lines.shape, jnp.int32),
            pltpu.VMEM(landed.shape, bf16),
            pltpu.VMEM((child_dev, BLK, 2 * HD), bf16),
            pltpu.VMEM((child_dev, BLK, 2 * HD), bf16),
            pltpu.SemaphoreType.DMA((2,)),
            pltpu.SemaphoreType.DMA((child_dev,)),
            pltpu.SemaphoreType.DMA((child_dev // GATHER,)),
        ],
        vmem=60,
        cost=(1000000, 8 * child_dev * BLK * 2 * HD, 0),
    )(matching_lines, all_tails.reshape(leaves, BLK, 2 * HD), landed)
    squares, children = lax.optimization_barrier((squares, children))
    branch = call(
        scale_kernel,
        shape((leaf_out, columns), bf16),
        [VMEM] * 3,
        VMEM,
    )(squares.reshape(nodes, HD), projected, post_gain.reshape(1, columns))
    return (branch, children.reshape(child_dev, BLK, 1, 2 * HD))


def solution(mesh):
    return jax.shard_map(
        shards,
        mesh=mesh,
        in_specs=(
            P(None, "node"),
            P("node", "head"),
            P("node", "head"),
            P("head", "node"),
            P("node"),
            P("node", None, "head", None),
            P("node", None, "head", None),
            P("node"),
            P(),
            P("node"),
            P(),
        ),
        out_specs=(P("head", "node"), P("node", None, "head", None)),
        check_vma=False,
    )
```

```python
import math

import jax
import jax.numpy as jnp
from jax import lax
from jax.experimental import pallas as pl
from jax.experimental.pallas import tpu as pltpu
from jax.sharding import PartitionSpec as P

D = 5376
HEADS = 32
KVH = 16
HD = 128
BLK = 64
GROUP = HEADS // KVH

score_scale = 168.0 ** (-0.5)
log2_scale = score_scale * math.log2(math.e)
neg_big = -1e30
epsilon = 1e-06
f32 = jnp.float32
bf16 = jnp.bfloat16
CHUNK = 3072
VROWS = HD + 16
GATHER = 8

VMEM = pl.BlockSpec(memory_space=pltpu.VMEM)
SMEM = pl.BlockSpec(memory_space=pltpu.SMEM)
HBM = pl.BlockSpec(memory_space=pltpu.HBM)


def call(kernel, out_shape, in_specs, out_specs, scratch=(), vmem=8, cost=(0, 0, 0)):
    return pl.pallas_call(
        kernel,
        out_shape=out_shape,
        in_specs=in_specs,
        out_specs=out_specs,
        scratch_shapes=list(scratch),
        compiler_params=pltpu.CompilerParams(vmem_limit_bytes=vmem * 1024 * 1024),
        cost_estimate=pl.CostEstimate(flops=cost[0], bytes_accessed=cost[1], transcendentals=cost[2]),
    )


def matmul_nt(a, b):
    return lax.dot_general(a, b, (((1,), (1,)), ((), ())), preferred_element_type=f32)


def identity(size):
    rows = lax.broadcasted_iota(jnp.int32, (size, size), 0)
    cols = lax.broadcasted_iota(jnp.int32, (size, size), 1)
    return (rows == cols).astype(f32).astype(bf16)


def halves(value):
    high = value.astype(bf16)
    return high, (value - high.astype(f32)).astype(bf16)


def project_kernel(
    states_hbm, query_hbm, key_value_hbm, matching_hbm, out, picks, states_t, w_query, w_key_value, matching, sems
):
    pairs = (
        (states_hbm, states_t),
        (query_hbm, w_query),
        (key_value_hbm, w_key_value),
        (matching_hbm, matching),
    )
    copies = [pltpu.make_async_copy(pair[0], pair[1], sems.at[i]) for i, pair in enumerate(pairs)]
    for copy in copies:
        copy.start()
    dims = (((0,), (0,)), ((), ()))
    cols = w_query.shape[1]
    for copy in copies:
        copy.wait()
    query = lax.dot_general(states_t[...], w_query[...], dims, preferred_element_type=f32)
    out[:, :cols], out[:, cols : 2 * cols] = halves(query)
    fresh = lax.dot_general(states_t[...], w_key_value[...], dims, preferred_element_type=f32)
    key, rest = halves(fresh[:, :HD])
    out[:, 2 * cols :] = jnp.concatenate([key, rest, fresh[:, HD:].astype(bf16)], axis=1)
    node = lax.axis_index("node")
    child_dev = matching.shape[0] * HD // lax.axis_size("node")
    leaf_dev = states_t.shape[1] // lax.axis_size("node")
    parent = matching[...]
    first = node * leaf_dev
    own = (parent >= first) & (parent < first + leaf_dev)
    part = jnp.where(own, parent - first, 0).astype(f32).astype(bf16)
    of = lax.broadcasted_iota(jnp.int32, (HD, HD), 0) // child_dev
    to = lax.broadcasted_iota(jnp.int32, (HD, HD), 1) // child_dev
    same = (of == to).astype(f32).astype(bf16)
    picks[...] = jnp.dot(part, same, preferred_element_type=f32).astype(jnp.int32)


def home_kernel(parts, query_rep, fresh):
    leaf_dev = fresh.shape[0]
    total = jnp.sum(parts[...].astype(f32).reshape(-1, leaf_dev, parts.shape[1]), axis=0)
    cols = GROUP * HD
    query = total[:, :cols] + total[:, cols : 2 * cols]
    pair = jnp.concatenate([query, query], axis=0).astype(bf16)
    for index in range(query_rep.shape[0] // 16):
        query_rep[pl.ds(index * 16, 16), :] = pair
    total = total[:, 2 * cols :]
    fresh[...] = jnp.concatenate([total[:, :HD] + total[:, HD : 2 * HD], total[:, 2 * HD :]], axis=1)


def leaf_lengths(lengths):
    lanes = lax.broadcasted_iota(jnp.int32, lengths.shape, 1)
    return [
        jnp.sum(jnp.where(lanes == leaf, lengths[...], 0).astype(f32), axis=1, keepdims=True)
        for leaf in range(lengths.shape[1])
    ]


def attend_kernel(
    rows_hbm,
    cache_hbm,
    tails_hbm,
    fresh_hbm,
    ancestry_hbm,
    block_node_hbm,
    lengths_hbm,
    picks_hbm,
    out,
    scores,
    values_t,
    updated,
    bias,
    cache,
    queries,
    tails,
    fresh,
    ancestry,
    block_node,
    lengths,
    picks,
    sems,
):
    node = lax.axis_index("node")
    nodes = out.shape[0]
    leaf_dev = lengths.shape[1]
    leaves = queries.shape[0]
    cached = cache.shape[0]
    steps = range(0, cached, CHUNK)
    pairs = [
        (ancestry_hbm, ancestry),
        (block_node_hbm, block_node),
        (lengths_hbm, lengths),
        (tails_hbm, tails),
        (fresh_hbm, fresh),
        (picks_hbm, picks),
        (rows_hbm, queries),
    ]
    pairs += [(cache_hbm.at[pl.ds(start, CHUNK), :], cache.at[pl.ds(start, CHUNK), :]) for start in steps]
    copies = [pltpu.make_async_copy(pair[0], pair[1], sems.at[i]) for i, pair in enumerate(pairs)]
    for copy in copies:
        copy.start()
    for copy in copies[:2]:
        copy.wait()
    nodes_all = ancestry.shape[1]
    tree = lax.broadcasted_iota(jnp.int32, (nodes_all, block_node.shape[1]), 0)
    one_hot = (tree == block_node[...]).astype(f32).astype(bf16)
    seen = lax.dot_general(
        one_hot,
        ancestry[...].astype(f32).astype(bf16),
        (((0,), (1,)), ((), ())),
        preferred_element_type=f32,
    )
    shut = jnp.where(seen > 0.5, 0.0, neg_big)
    for g in range(GROUP):
        bias[:, g * leaves : (g + 1) * leaves] = shut
    eye = identity(HD)
    values_t[HD:, :] = jnp.ones((VROWS - HD, values_t.shape[1]), bf16)
    for copy in copies[2:6]:
        copy.wait()
    length = leaf_lengths(lengths)
    rows = lax.broadcasted_iota(jnp.int32, (BLK, 2 * HD), 0).astype(f32)
    for leaf in range(leaf_dev):
        span = pl.ds(leaf * BLK, BLK)
        block = jnp.where(rows < length[leaf], tails[span, :].astype(f32), 0.0)
        block = jnp.where(rows == length[leaf], fresh[leaf : leaf + 1, :], block)
        updated[span, :] = block.astype(bf16)
    values_t[:HD, cached:] = matmul_nt(eye, updated[:, HD:]).astype(bf16)
    rows_all = leaves * GROUP
    copies[6].wait()
    query = jnp.concatenate([queries[:, HD * g : HD * (g + 1)] for g in range(GROUP)], axis=0)
    own = updated.shape[0]
    top = jnp.full((8, rows_all), neg_big, f32)
    lanes = lax.broadcasted_iota(jnp.int32, (BLK, rows_all), 1) % leaves
    rows = lax.broadcasted_iota(jnp.int32, (BLK, rows_all), 0).astype(f32)
    raw = matmul_nt(updated[:, :HD], query)
    for leaf in range(leaf_dev):
        keep = (lanes == node * leaf_dev + leaf) & (rows <= length[leaf])
        part = jnp.where(keep, raw[leaf * BLK : (leaf + 1) * BLK] * log2_scale, neg_big)
        scores[pl.ds(cached + leaf * BLK, BLK), :] = part
        top = jnp.maximum(top, jnp.max(part.reshape(BLK // 8, 8, rows_all), axis=0))
    for step, start in enumerate(steps):
        copies[7 + step].wait()
        values_t[:HD, start : start + CHUNK] = matmul_nt(eye, cache[start : start + CHUNK, HD:]).astype(bf16)
        raw = matmul_nt(cache[start : start + CHUNK, :HD], query)
        for block in range(CHUNK // BLK):
            at = start // BLK + block
            part = raw[block * BLK : (block + 1) * BLK] * log2_scale + bias[at : at + 1, :]
            scores[pl.ds(start + block * BLK, BLK), :] = part
            top = jnp.maximum(top, jnp.max(part.reshape(BLK // 8, 8, rows_all), axis=0))
    row_max = jnp.max(top, axis=0, keepdims=True)
    total = jnp.zeros((VROWS, rows_all), f32)
    for start in range(0, cached + own, CHUNK):
        stop = min(start + CHUNK, cached + own)
        weights = jnp.exp2(scores[start:stop, :] - row_max).astype(bf16)
        total = total + jnp.dot(values_t[:, start:stop], weights, preferred_element_type=f32)
    weight_sum = total[HD : HD + 1]
    mean_t = (total[:HD] / weight_sum).astype(bf16)
    level = row_max + jnp.log2(weight_sum)
    high = level.astype(bf16).astype(f32)
    middle = (level - high).astype(bf16).astype(f32)
    low = level - high - middle
    lines = (nodes * 8, rows_all)
    line = lax.broadcasted_iota(jnp.int32, lines, 0)
    row = lax.broadcasted_iota(jnp.int32, lines, 1)
    part = line % 8
    level = jnp.where(part == 0, high, jnp.where(part == 1, middle, jnp.where(part == 2, low, 0.0)))
    level = jnp.where(row % leaves // leaf_dev == line // 8, level, 0.0).astype(bf16)
    row = lax.broadcasted_iota(jnp.int32, (rows_all, HD), 0)
    lane = lax.broadcasted_iota(jnp.int32, (rows_all, HD), 1)
    gather = (row // leaves * leaf_dev + row % leaf_dev == lane).astype(f32).astype(bf16)
    levels = jnp.dot(level, gather, preferred_element_type=f32)
    line = lax.broadcasted_iota(jnp.int32, (nodes * 8, picks.shape[0]), 0)
    spot = lax.broadcasted_iota(jnp.int32, (nodes * 8, picks.shape[0]), 1)
    per_line = nodes // picks.shape[0]
    lift = (line // (8 * per_line) == spot).astype(f32).astype(bf16)
    pick = jnp.dot(lift, picks[...].astype(f32).astype(bf16), preferred_element_type=f32)
    line = lax.broadcasted_iota(jnp.int32, pick.shape, 0)
    lane = lax.broadcasted_iota(jnp.int32, pick.shape, 1)
    chosen = lane == line // 8 % per_line * (HD // per_line)
    pick = jnp.sum(jnp.where(chosen, pick, 0.0), axis=1, keepdims=True)
    line = lax.broadcasted_iota(jnp.int32, (nodes * 8, 3 * leaf_dev), 0)
    of = lax.broadcasted_iota(jnp.int32, (nodes * 8, 3 * leaf_dev), 1)
    hit = (of % leaf_dev == pick.astype(jnp.int32)) & (of // leaf_dev == line % 8 - 3)
    sizes = jnp.concatenate([jnp.broadcast_to(value, (1, HD)) for value in length], axis=0)
    source = jnp.concatenate([sizes, fresh[:, :HD], fresh[:, HD:]], axis=0).astype(bf16)
    levels = levels + jnp.dot(hit.astype(f32).astype(bf16), source, preferred_element_type=f32)
    levels = levels.reshape(nodes, 8, HD)
    eye = identity(leaves)
    turned = [
        matmul_nt(eye, mean_t[:, g * leaves : (g + 1) * leaves]).reshape(nodes, leaf_dev, HD)
        for g in range(GROUP)
    ]
    out[...] = jnp.concatenate(turned + [levels], axis=1).astype(bf16)


def combine_kernel(parts, out):
    nodes = parts.shape[0]
    leaf_dev = out.shape[0] // nodes
    span = GROUP * leaf_dev
    both = parts[...].astype(f32)
    mean = both[:, :span, :]
    lines = both[:, span:, :].reshape(nodes * 8, HD).astype(bf16)
    row = lax.broadcasted_iota(jnp.int32, (nodes * span, nodes * 8), 0)
    line = lax.broadcasted_iota(jnp.int32, (nodes * span, nodes * 8), 1)
    spread = ((row // span == line // 8) & (line % 8 < 3)).astype(f32).astype(bf16)
    level = jnp.dot(spread, lines, preferred_element_type=f32).reshape(nodes, span, HD)
    own = lax.broadcasted_iota(jnp.int32, level.shape, 2) == lax.broadcasted_iota(jnp.int32, level.shape, 1)
    level = jnp.sum(jnp.where(own, level, 0.0), axis=2, keepdims=True)
    top = jnp.max(level, axis=0, keepdims=True)
    weight = jnp.broadcast_to(jnp.exp2(level - top), mean.shape)
    result = jnp.sum(weight * mean, axis=0) / jnp.sum(weight, axis=0)
    mine = jnp.concatenate([result[g * leaf_dev : (g + 1) * leaf_dev] for g in range(GROUP)], axis=1)
    pair = jnp.concatenate([mine, mine], axis=0).astype(bf16)
    for index in range(out.shape[0] // 16):
        out[pl.ds(index * 16, 16), :] = pair


def output_kernel(attention, w_out_t, partial):
    partial[...] = matmul_nt(attention[...], w_out_t[...]).astype(bf16)


def square_kernel(partial, projected, squares):
    total = jnp.sum(partial[...].astype(f32), axis=0)
    projected[...] = total
    sums = jnp.sum(total * total, axis=1, keepdims=True)
    leaves = total.shape[0]
    rows = lax.broadcasted_iota(jnp.int32, (leaves, HD), 0)
    cols = lax.broadcasted_iota(jnp.int32, (leaves, HD), 1)
    line = jnp.sum(jnp.where(rows == cols, sums, 0.0), axis=0, keepdims=True)
    squares[...] = jnp.broadcast_to(line, squares.shape)


def scale_kernel(squares, projected, gain, branch):
    leaves = projected.shape[0]
    line = jnp.sum(squares[...], axis=0, keepdims=True)
    rows = lax.broadcasted_iota(jnp.int32, (leaves, HD), 0)
    cols = lax.broadcasted_iota(jnp.int32, (leaves, HD), 1)
    sums = jnp.sum(jnp.where(rows == cols, line, 0.0), axis=1, keepdims=True)
    inverse = lax.rsqrt(sums / D + epsilon)
    branch[...] = (projected[...] * inverse * gain[...]).astype(bf16)


def children_kernel(
    matching_hbm, tails, landed_hbm, out, matching, landed, blocks, built, sems, in_sems, out_sems
):
    node = lax.axis_index("node")
    count = out.shape[0]
    leaf_dev = tails.shape[0] // landed.shape[0]
    table = pltpu.make_async_copy(matching_hbm, matching, sems.at[0])
    table.start()
    extra = pltpu.make_async_copy(landed_hbm, landed, sems.at[1])
    extra.start()
    table.wait()
    parents = []
    fetches = []
    for index in range(count):
        place = node * count + index
        parent = matching[place // HD, place % HD]
        copy = pltpu.make_async_copy(tails.at[parent], blocks.at[index], in_sems.at[index])
        copy.start()
        parents.append(parent)
        fetches.append(copy)
    extra.wait()
    rows = lax.broadcasted_iota(jnp.int32, (BLK, 2 * HD), 0).astype(f32)
    span = landed.shape[1] - 8
    lengths = []
    fresh = []
    for parent in parents:
        lines = landed[parent // leaf_dev].astype(f32)[span:]
        lengths.append(jnp.broadcast_to(lines[3:4, 0:1], (1, 2 * HD)))
        fresh.append(jnp.concatenate([lines[4:5], lines[5:6]], axis=1))
    stores = []
    for first in range(0, count, GATHER):
        group = range(first, first + GATHER)
        for index in group:
            fetches[index].wait()
        for index in group:
            block = jnp.where(rows < lengths[index], blocks[index].astype(f32), 0.0)
            built[index] = jnp.where(rows == lengths[index], fresh[index], block).astype(bf16)
        copy = pltpu.make_async_copy(
            built.at[pl.ds(first, GATHER)], out.at[pl.ds(first, GATHER)], out_sems.at[first // GATHER]
        )
        copy.start()
        stores.append(copy)
    for copy in stores:
        copy.wait()


def shards(
    states,
    w_query,
    w_key_value,
    w_out,
    post_gain,
    cache,
    tails,
    lengths,
    ancestry,
    block_node,
    matching,
):
    nodes = lax.axis_size("node")
    heads = lax.axis_size("head")
    leaves = states.shape[0]
    leaf_dev = leaves // nodes
    query_cols = w_query.shape[1]
    all_cols = 2 * query_cols + 3 * HD
    columns = w_out.shape[1]
    rows_all = leaves * GROUP
    child_dev = matching.shape[0] // nodes
    shape = jax.ShapeDtypeStruct

    cache_rows = cache.reshape(-1, 2 * HD)
    tail_rows = tails.reshape(-1, 2 * HD)
    key_count = cache_rows.shape[0]
    extended = key_count + leaf_dev * BLK
    all_tails = lax.all_gather(tail_rows, "node", axis=0, tiled=True)
    matching_lines = matching.reshape(-1, HD)
    length_line = lengths.reshape(1, -1)

    partial, picks = call(
        project_kernel,
        (shape((leaves, all_cols), bf16), shape(matching_lines.shape, jnp.int32)),
        [HBM] * 4,
        (VMEM, VMEM),
        [
            pltpu.VMEM((states.shape[1], leaves), bf16),
            pltpu.VMEM(w_query.shape, bf16),
            pltpu.VMEM(w_key_value.shape, bf16),
            pltpu.VMEM(matching_lines.shape, jnp.int32),
            pltpu.SemaphoreType.DMA((4,)),
        ],
        vmem=60,
        cost=(2 * leaves * all_cols * states.shape[1], 1000000, 0),
    )(states.T, w_query, w_key_value, matching_lines)
    parts = lax.all_to_all(partial.reshape(nodes, leaf_dev, all_cols), "node", 0, 0, tiled=True)

    parts = parts.reshape(leaves, all_cols)
    query_rep, fresh = call(
        home_kernel,
        (shape((leaves, query_cols), bf16), shape((leaf_dev, 2 * HD), f32)),
        [VMEM],
        (VMEM, VMEM),
        cost=(leaves * all_cols, 4 * leaves * all_cols, 0),
    )(parts)
    rows = lax.all_to_all(query_rep.reshape(nodes, leaf_dev, query_cols), "node", 0, 0, tiled=True)

    span = GROUP * leaf_dev + 8
    sent = call(
        attend_kernel,
        shape((nodes, span, HD), bf16),
        [HBM] * 8,
        VMEM,
        [
            pltpu.VMEM((extended, rows_all), f32),
            pltpu.VMEM((VROWS, extended), bf16),
            pltpu.VMEM((leaf_dev * BLK, 2 * HD), bf16),
            pltpu.VMEM((block_node.shape[0], rows_all), f32),
            pltpu.VMEM(cache_rows.shape, bf16),
            pltpu.VMEM((leaves, query_cols), bf16),
            pltpu.VMEM(tail_rows.shape, bf16),
            pltpu.VMEM(fresh.shape, f32),
            pltpu.VMEM(ancestry.shape, jnp.int32),
            pltpu.VMEM((1, block_node.shape[0]), jnp.int32),
            pltpu.VMEM((1, leaf_dev), jnp.int32),
            pltpu.VMEM(picks.shape, jnp.int32),
            pltpu.SemaphoreType.DMA((7 + key_count // CHUNK,)),
        ],
        vmem=60,
        cost=(4 * rows_all * extended * HD, 8 * HD * key_count, rows_all * extended),
    )(
        rows.reshape(leaves, query_cols),
        cache_rows,
        tail_rows,
        fresh,
        ancestry,
        block_node.reshape(1, -1),
        length_line,
        picks,
    )
    landed = lax.all_to_all(sent, "node", 0, 0, tiled=True)
    mine = call(
        combine_kernel,
        shape((leaves, query_cols), bf16),
        [VMEM],
        VMEM,
        cost=(10 * rows_all * HD, 4 * rows_all * HD, rows_all * HD),
    )(landed)
    attention = lax.all_to_all(mine.reshape(nodes, leaf_dev, query_cols), "node", 0, 0, tiled=True)
    leaf_out = leaves // heads
    partial_out = call(
        output_kernel,
        shape((leaves, columns), bf16),
        [VMEM, VMEM],
        VMEM,
        cost=(2 * leaves * columns * query_cols, 6 * columns * query_cols, 0),
    )(attention.reshape(leaves, query_cols), w_out.T)
    partial_out = lax.all_to_all(
        partial_out.reshape(heads, leaf_out, columns), "head", 0, 0, tiled=True
    )
    projected, squares = call(
        square_kernel,
        (shape((leaf_out, columns), f32), shape((nodes, HD), f32)),
        [VMEM],
        (VMEM, VMEM),
        cost=(leaves * columns, 4 * leaves * columns, 0),
    )(partial_out)
    squares = lax.all_to_all(squares.reshape(nodes, 1, HD), "node", 0, 0, tiled=True)
    children = call(
        children_kernel,
        shape((child_dev, BLK, 2 * HD), bf16),
        [HBM] * 3,
        HBM,
        [
            pltpu.SMEM(matching_lines.shape, jnp.int32),
            pltpu.VMEM(landed.shape, bf16),
            pltpu.VMEM((child_dev, BLK, 2 * HD), bf16),
            pltpu.VMEM((child_dev, BLK, 2 * HD), bf16),
            pltpu.SemaphoreType.DMA((2,)),
            pltpu.SemaphoreType.DMA((child_dev,)),
            pltpu.SemaphoreType.DMA((child_dev // GATHER,)),
        ],
        vmem=60,
        cost=(1000000, 8 * child_dev * BLK * 2 * HD, 0),
    )(matching_lines, all_tails.reshape(leaves, BLK, 2 * HD), landed)
    squares, children = lax.optimization_barrier((squares, children))
    branch = call(
        scale_kernel,
        shape((leaf_out, columns), bf16),
        [VMEM] * 3,
        VMEM,
    )(squares.reshape(nodes, HD), projected, post_gain.reshape(1, columns))
    return (branch, children.reshape(child_dev, BLK, 1, 2 * HD))


def solution(mesh):
    return jax.shard_map(
        shards,
        mesh=mesh,
        in_specs=(
            P(None, "node"),
            P("node", "head"),
            P("node", "head"),
            P("head", "node"),
            P("node"),
            P("node", None, "head", None),
            P("node", None, "head", None),
            P("node"),
            P(),
            P("node"),
            P(),
        ),
        out_specs=(P("head", "node"), P("node", None, "head", None)),
        check_vma=False,
    )
```

```python
import math

import jax
import jax.numpy as jnp
from jax import lax
from jax.experimental import pallas as pl
from jax.experimental.pallas import tpu as pltpu
from jax.sharding import PartitionSpec as P

D = 5376
HEADS = 32
KVH = 16
HD = 128
BLK = 64
GROUP = HEADS // KVH

score_scale = 168.0 ** (-0.5)
log2_scale = score_scale * math.log2(math.e)
neg_big = -1e30
epsilon = 1e-06
f32 = jnp.float32
bf16 = jnp.bfloat16
CHUNK = 3072
VROWS = HD + 16
GATHER = 8

VMEM = pl.BlockSpec(memory_space=pltpu.VMEM)
SMEM = pl.BlockSpec(memory_space=pltpu.SMEM)
HBM = pl.BlockSpec(memory_space=pltpu.HBM)


def call(kernel, out_shape, in_specs, out_specs, scratch=(), vmem=8, cost=(0, 0, 0)):
    return pl.pallas_call(
        kernel,
        out_shape=out_shape,
        in_specs=in_specs,
        out_specs=out_specs,
        scratch_shapes=list(scratch),
        compiler_params=pltpu.CompilerParams(vmem_limit_bytes=vmem * 1024 * 1024),
        cost_estimate=pl.CostEstimate(flops=cost[0], bytes_accessed=cost[1], transcendentals=cost[2]),
    )


def matmul_nt(a, b):
    return lax.dot_general(a, b, (((1,), (1,)), ((), ())), preferred_element_type=f32)


def identity(size):
    rows = lax.broadcasted_iota(jnp.int32, (size, size), 0)
    cols = lax.broadcasted_iota(jnp.int32, (size, size), 1)
    return (rows == cols).astype(f32).astype(bf16)


def halves(value):
    high = value.astype(bf16)
    return high, (value - high.astype(f32)).astype(bf16)


def project_kernel(
    states_hbm, query_hbm, key_value_hbm, out, states_t, w_query, w_key_value, sems
):
    pairs = (
        (states_hbm, states_t),
        (query_hbm, w_query),
        (key_value_hbm, w_key_value),
    )
    copies = [pltpu.make_async_copy(pair[0], pair[1], sems.at[i]) for i, pair in enumerate(pairs)]
    for copy in copies:
        copy.start()
    dims = (((0,), (0,)), ((), ()))
    cols = w_query.shape[1]
    for copy in copies:
        copy.wait()
    query = lax.dot_general(states_t[...], w_query[...], dims, preferred_element_type=f32)
    out[:, :cols], out[:, cols : 2 * cols] = halves(query)
    fresh = lax.dot_general(states_t[...], w_key_value[...], dims, preferred_element_type=f32)
    key, rest = halves(fresh[:, :HD])
    out[:, 2 * cols :] = jnp.concatenate([key, rest, fresh[:, HD:].astype(bf16)], axis=1)


def home_kernel(parts, query_rep, fresh):
    leaf_dev = fresh.shape[0]
    total = jnp.sum(parts[...].astype(f32).reshape(-1, leaf_dev, parts.shape[1]), axis=0)
    cols = GROUP * HD
    query = total[:, :cols] + total[:, cols : 2 * cols]
    pair = jnp.concatenate([query, query], axis=0).astype(bf16)
    for index in range(query_rep.shape[0] // 16):
        query_rep[pl.ds(index * 16, 16), :] = pair
    total = total[:, 2 * cols :]
    fresh[...] = jnp.concatenate([total[:, :HD] + total[:, HD : 2 * HD], total[:, 2 * HD :]], axis=1)


def leaf_lengths(lengths):
    lanes = lax.broadcasted_iota(jnp.int32, lengths.shape, 1)
    return [
        jnp.sum(jnp.where(lanes == leaf, lengths[...], 0).astype(f32), axis=1, keepdims=True)
        for leaf in range(lengths.shape[1])
    ]


def attend_kernel(
    rows_hbm,
    cache_hbm,
    tails_hbm,
    fresh_hbm,
    ancestry_hbm,
    block_node_hbm,
    lengths_hbm,
    matching_hbm,
    out,
    scores,
    values_t,
    updated,
    bias,
    cache,
    queries,
    tails,
    fresh,
    ancestry,
    block_node,
    lengths,
    matching,
    sems,
):
    node = lax.axis_index("node")
    nodes = out.shape[0]
    leaf_dev = lengths.shape[1]
    leaves = queries.shape[0]
    cached = cache.shape[0]
    steps = range(0, cached, CHUNK)
    pairs = [
        (ancestry_hbm, ancestry),
        (block_node_hbm, block_node),
        (lengths_hbm, lengths),
        (tails_hbm, tails),
        (fresh_hbm, fresh),
        (matching_hbm, matching),
        (rows_hbm, queries),
    ]
    pairs += [(cache_hbm.at[pl.ds(start, CHUNK), :], cache.at[pl.ds(start, CHUNK), :]) for start in steps]
    copies = [pltpu.make_async_copy(pair[0], pair[1], sems.at[i]) for i, pair in enumerate(pairs)]
    for copy in copies:
        copy.start()
    for copy in copies[:2]:
        copy.wait()
    nodes_all = ancestry.shape[1]
    tree = lax.broadcasted_iota(jnp.int32, (nodes_all, block_node.shape[1]), 0)
    one_hot = (tree == block_node[...]).astype(f32).astype(bf16)
    seen = lax.dot_general(
        one_hot,
        ancestry[...].astype(f32).astype(bf16),
        (((0,), (1,)), ((), ())),
        preferred_element_type=f32,
    )
    shut = jnp.where(seen > 0.5, 0.0, neg_big)
    for g in range(GROUP):
        bias[:, g * leaves : (g + 1) * leaves] = shut
    eye = identity(HD)
    values_t[HD:, :] = jnp.ones((VROWS - HD, values_t.shape[1]), bf16)
    for copy in copies[2:6]:
        copy.wait()
    length = leaf_lengths(lengths)
    child_dev = matching.shape[0] * HD // nodes
    parent = matching[...]
    first = node * leaf_dev
    mine = (parent >= first) & (parent < first + leaf_dev)
    part = jnp.where(mine, parent - first, 0).astype(f32).astype(bf16)
    of = lax.broadcasted_iota(jnp.int32, (HD, HD), 0) // child_dev
    to = lax.broadcasted_iota(jnp.int32, (HD, HD), 1) // child_dev
    same = (of == to).astype(f32).astype(bf16)
    picks = jnp.dot(part, same, preferred_element_type=f32).astype(bf16)
    rows = lax.broadcasted_iota(jnp.int32, (BLK, 2 * HD), 0).astype(f32)
    for leaf in range(leaf_dev):
        span = pl.ds(leaf * BLK, BLK)
        block = jnp.where(rows < length[leaf], tails[span, :].astype(f32), 0.0)
        block = jnp.where(rows == length[leaf], fresh[leaf : leaf + 1, :], block)
        updated[span, :] = block.astype(bf16)
    values_t[:HD, cached:] = matmul_nt(eye, updated[:, HD:]).astype(bf16)
    rows_all = leaves * GROUP
    copies[6].wait()
    query = jnp.concatenate([queries[:, HD * g : HD * (g + 1)] for g in range(GROUP)], axis=0)
    own = updated.shape[0]
    top = jnp.full((8, rows_all), neg_big, f32)
    lanes = lax.broadcasted_iota(jnp.int32, (BLK, rows_all), 1) % leaves
    rows = lax.broadcasted_iota(jnp.int32, (BLK, rows_all), 0).astype(f32)
    raw = matmul_nt(updated[:, :HD], query)
    for leaf in range(leaf_dev):
        keep = (lanes == node * leaf_dev + leaf) & (rows <= length[leaf])
        part = jnp.where(keep, raw[leaf * BLK : (leaf + 1) * BLK] * log2_scale, neg_big)
        scores[pl.ds(cached + leaf * BLK, BLK), :] = part
        top = jnp.maximum(top, jnp.max(part.reshape(BLK // 8, 8, rows_all), axis=0))
    for step, start in enumerate(steps):
        copies[7 + step].wait()
        values_t[:HD, start : start + CHUNK] = matmul_nt(eye, cache[start : start + CHUNK, HD:]).astype(bf16)
        raw = matmul_nt(cache[start : start + CHUNK, :HD], query)
        for block in range(CHUNK // BLK):
            at = start // BLK + block
            part = raw[block * BLK : (block + 1) * BLK] * log2_scale + bias[at : at + 1, :]
            scores[pl.ds(start + block * BLK, BLK), :] = part
            top = jnp.maximum(top, jnp.max(part.reshape(BLK // 8, 8, rows_all), axis=0))
    row_max = jnp.max(top, axis=0, keepdims=True)
    total = jnp.zeros((VROWS, rows_all), f32)
    for start in range(0, cached + own, CHUNK):
        stop = min(start + CHUNK, cached + own)
        weights = jnp.exp2(scores[start:stop, :] - row_max).astype(bf16)
        total = total + jnp.dot(values_t[:, start:stop], weights, preferred_element_type=f32)
    weight_sum = total[HD : HD + 1]
    mean_t = (total[:HD] / weight_sum).astype(bf16)
    level = row_max + jnp.log2(weight_sum)
    high = level.astype(bf16).astype(f32)
    middle = (level - high).astype(bf16).astype(f32)
    low = level - high - middle
    lines = (nodes * 8, rows_all)
    line = lax.broadcasted_iota(jnp.int32, lines, 0)
    row = lax.broadcasted_iota(jnp.int32, lines, 1)
    part = line % 8
    level = jnp.where(part == 0, high, jnp.where(part == 1, middle, jnp.where(part == 2, low, 0.0)))
    level = jnp.where(row % leaves // leaf_dev == line // 8, level, 0.0).astype(bf16)
    row = lax.broadcasted_iota(jnp.int32, (rows_all, HD), 0)
    lane = lax.broadcasted_iota(jnp.int32, (rows_all, HD), 1)
    gather = (row // leaves * leaf_dev + row % leaf_dev == lane).astype(f32).astype(bf16)
    levels = jnp.dot(level, gather, preferred_element_type=f32)
    line = lax.broadcasted_iota(jnp.int32, (nodes * 8, picks.shape[0]), 0)
    spot = lax.broadcasted_iota(jnp.int32, (nodes * 8, picks.shape[0]), 1)
    per_line = nodes // picks.shape[0]
    lift = (line // (8 * per_line) == spot).astype(f32).astype(bf16)
    pick = jnp.dot(lift, picks, preferred_element_type=f32)
    line = lax.broadcasted_iota(jnp.int32, pick.shape, 0)
    lane = lax.broadcasted_iota(jnp.int32, pick.shape, 1)
    chosen = lane == line // 8 % per_line * (HD // per_line)
    pick = jnp.sum(jnp.where(chosen, pick, 0.0), axis=1, keepdims=True)
    line = lax.broadcasted_iota(jnp.int32, (nodes * 8, 3 * leaf_dev), 0)
    of = lax.broadcasted_iota(jnp.int32, (nodes * 8, 3 * leaf_dev), 1)
    hit = (of % leaf_dev == pick.astype(jnp.int32)) & (of // leaf_dev == line % 8 - 3)
    sizes = jnp.concatenate([jnp.broadcast_to(value, (1, HD)) for value in length], axis=0)
    source = jnp.concatenate([sizes, fresh[:, :HD], fresh[:, HD:]], axis=0).astype(bf16)
    levels = levels + jnp.dot(hit.astype(f32).astype(bf16), source, preferred_element_type=f32)
    levels = levels.reshape(nodes, 8, HD)
    eye = identity(leaves)
    turned = [
        matmul_nt(eye, mean_t[:, g * leaves : (g + 1) * leaves]).reshape(nodes, leaf_dev, HD)
        for g in range(GROUP)
    ]
    out[...] = jnp.concatenate(turned + [levels], axis=1).astype(bf16)


def combine_kernel(parts, out):
    nodes = parts.shape[0]
    leaf_dev = out.shape[0] // nodes
    span = GROUP * leaf_dev
    both = parts[...].astype(f32)
    mean = both[:, :span, :]
    lines = both[:, span:, :].reshape(nodes * 8, HD).astype(bf16)
    row = lax.broadcasted_iota(jnp.int32, (nodes * span, nodes * 8), 0)
    line = lax.broadcasted_iota(jnp.int32, (nodes * span, nodes * 8), 1)
    spread = ((row // span == line // 8) & (line % 8 < 3)).astype(f32).astype(bf16)
    level = jnp.dot(spread, lines, preferred_element_type=f32).reshape(nodes, span, HD)
    own = lax.broadcasted_iota(jnp.int32, level.shape, 2) == lax.broadcasted_iota(jnp.int32, level.shape, 1)
    level = jnp.sum(jnp.where(own, level, 0.0), axis=2, keepdims=True)
    top = jnp.max(level, axis=0, keepdims=True)
    weight = jnp.broadcast_to(jnp.exp2(level - top), mean.shape)
    result = jnp.sum(weight * mean, axis=0) / jnp.sum(weight, axis=0)
    mine = jnp.concatenate([result[g * leaf_dev : (g + 1) * leaf_dev] for g in range(GROUP)], axis=1)
    pair = jnp.concatenate([mine, mine], axis=0).astype(bf16)
    for index in range(out.shape[0] // 16):
        out[pl.ds(index * 16, 16), :] = pair


def output_kernel(attention, w_out_t, partial):
    partial[...] = matmul_nt(attention[...], w_out_t[...]).astype(bf16)


def square_kernel(partial, projected, squares):
    total = jnp.sum(partial[...].astype(f32), axis=0)
    projected[...] = total
    sums = jnp.sum(total * total, axis=1, keepdims=True)
    leaves = total.shape[0]
    rows = lax.broadcasted_iota(jnp.int32, (leaves, HD), 0)
    cols = lax.broadcasted_iota(jnp.int32, (leaves, HD), 1)
    line = jnp.sum(jnp.where(rows == cols, sums, 0.0), axis=0, keepdims=True)
    squares[...] = jnp.broadcast_to(line, squares.shape)


def scale_kernel(squares, projected, gain, branch):
    leaves = projected.shape[0]
    line = jnp.sum(squares[...], axis=0, keepdims=True)
    rows = lax.broadcasted_iota(jnp.int32, (leaves, HD), 0)
    cols = lax.broadcasted_iota(jnp.int32, (leaves, HD), 1)
    sums = jnp.sum(jnp.where(rows == cols, line, 0.0), axis=1, keepdims=True)
    inverse = lax.rsqrt(sums / D + epsilon)
    branch[...] = (projected[...] * inverse * gain[...]).astype(bf16)


def children_kernel(
    matching_hbm, tails, landed_hbm, out, matching, landed, blocks, built, sems, in_sems, out_sems
):
    node = lax.axis_index("node")
    count = out.shape[0]
    leaf_dev = tails.shape[0] // landed.shape[0]
    table = pltpu.make_async_copy(matching_hbm, matching, sems.at[0])
    table.start()
    extra = pltpu.make_async_copy(landed_hbm, landed, sems.at[1])
    extra.start()
    table.wait()
    parents = []
    fetches = []
    for index in range(count):
        place = node * count + index
        parent = matching[place // HD, place % HD]
        copy = pltpu.make_async_copy(tails.at[parent], blocks.at[index], in_sems.at[index])
        copy.start()
        parents.append(parent)
        fetches.append(copy)
    extra.wait()
    rows = lax.broadcasted_iota(jnp.int32, (BLK, 2 * HD), 0).astype(f32)
    span = landed.shape[1] - 8
    lengths = []
    fresh = []
    for parent in parents:
        lines = landed[parent // leaf_dev].astype(f32)[span:]
        lengths.append(jnp.broadcast_to(lines[3:4, 0:1], (1, 2 * HD)))
        fresh.append(jnp.concatenate([lines[4:5], lines[5:6]], axis=1))
    stores = []
    for first in range(0, count, GATHER):
        group = range(first, first + GATHER)
        for index in group:
            fetches[index].wait()
        for index in group:
            block = jnp.where(rows < lengths[index], blocks[index].astype(f32), 0.0)
            built[index] = jnp.where(rows == lengths[index], fresh[index], block).astype(bf16)
        copy = pltpu.make_async_copy(
            built.at[pl.ds(first, GATHER)], out.at[pl.ds(first, GATHER)], out_sems.at[first // GATHER]
        )
        copy.start()
        stores.append(copy)
    for copy in stores:
        copy.wait()


def shards(
    states,
    w_query,
    w_key_value,
    w_out,
    post_gain,
    cache,
    tails,
    lengths,
    ancestry,
    block_node,
    matching,
):
    nodes = lax.axis_size("node")
    heads = lax.axis_size("head")
    leaves = states.shape[0]
    leaf_dev = leaves // nodes
    query_cols = w_query.shape[1]
    all_cols = 2 * query_cols + 3 * HD
    columns = w_out.shape[1]
    rows_all = leaves * GROUP
    child_dev = matching.shape[0] // nodes
    shape = jax.ShapeDtypeStruct

    cache_rows = cache.reshape(-1, 2 * HD)
    tail_rows = tails.reshape(-1, 2 * HD)
    key_count = cache_rows.shape[0]
    extended = key_count + leaf_dev * BLK
    all_tails = lax.all_gather(tail_rows, "node", axis=0, tiled=True)
    matching_lines = matching.reshape(-1, HD)
    length_line = lengths.reshape(1, -1)

    partial = call(
        project_kernel,
        shape((leaves, all_cols), bf16),
        [HBM] * 3,
        VMEM,
        [
            pltpu.VMEM((states.shape[1], leaves), bf16),
            pltpu.VMEM(w_query.shape, bf16),
            pltpu.VMEM(w_key_value.shape, bf16),
            pltpu.SemaphoreType.DMA((3,)),
        ],
        vmem=60,
        cost=(2 * leaves * all_cols * states.shape[1], 1000000, 0),
    )(states.T, w_query, w_key_value)
    parts = lax.all_to_all(partial.reshape(nodes, leaf_dev, all_cols), "node", 0, 0, tiled=True)

    parts = parts.reshape(leaves, all_cols)
    query_rep, fresh = call(
        home_kernel,
        (shape((leaves, query_cols), bf16), shape((leaf_dev, 2 * HD), f32)),
        [VMEM],
        (VMEM, VMEM),
        cost=(leaves * all_cols, 4 * leaves * all_cols, 0),
    )(parts)
    rows = lax.all_to_all(query_rep.reshape(nodes, leaf_dev, query_cols), "node", 0, 0, tiled=True)

    span = GROUP * leaf_dev + 8
    sent = call(
        attend_kernel,
        shape((nodes, span, HD), bf16),
        [HBM] * 8,
        VMEM,
        [
            pltpu.VMEM((extended, rows_all), f32),
            pltpu.VMEM((VROWS, extended), bf16),
            pltpu.VMEM((leaf_dev * BLK, 2 * HD), bf16),
            pltpu.VMEM((block_node.shape[0], rows_all), f32),
            pltpu.VMEM(cache_rows.shape, bf16),
            pltpu.VMEM((leaves, query_cols), bf16),
            pltpu.VMEM(tail_rows.shape, bf16),
            pltpu.VMEM(fresh.shape, f32),
            pltpu.VMEM(ancestry.shape, jnp.int32),
            pltpu.VMEM((1, block_node.shape[0]), jnp.int32),
            pltpu.VMEM((1, leaf_dev), jnp.int32),
            pltpu.VMEM(matching_lines.shape, jnp.int32),
            pltpu.SemaphoreType.DMA((7 + key_count // CHUNK,)),
        ],
        vmem=60,
        cost=(4 * rows_all * extended * HD, 8 * HD * key_count, rows_all * extended),
    )(
        rows.reshape(leaves, query_cols),
        cache_rows,
        tail_rows,
        fresh,
        ancestry,
        block_node.reshape(1, -1),
        length_line,
        matching_lines,
    )
    landed = lax.all_to_all(sent, "node", 0, 0, tiled=True)
    mine = call(
        combine_kernel,
        shape((leaves, query_cols), bf16),
        [VMEM],
        VMEM,
        cost=(10 * rows_all * HD, 4 * rows_all * HD, rows_all * HD),
    )(landed)
    attention = lax.all_to_all(mine.reshape(nodes, leaf_dev, query_cols), "node", 0, 0, tiled=True)
    leaf_out = leaves // heads
    partial_out = call(
        output_kernel,
        shape((leaves, columns), bf16),
        [VMEM, VMEM],
        VMEM,
        cost=(2 * leaves * columns * query_cols, 6 * columns * query_cols, 0),
    )(attention.reshape(leaves, query_cols), w_out.T)
    partial_out = lax.all_to_all(
        partial_out.reshape(heads, leaf_out, columns), "head", 0, 0, tiled=True
    )
    projected, squares = call(
        square_kernel,
        (shape((leaf_out, columns), f32), shape((nodes, HD), f32)),
        [VMEM],
        (VMEM, VMEM),
        cost=(leaves * columns, 4 * leaves * columns, 0),
    )(partial_out)
    squares = lax.all_to_all(squares.reshape(nodes, 1, HD), "node", 0, 0, tiled=True)
    children = call(
        children_kernel,
        shape((child_dev, BLK, 2 * HD), bf16),
        [HBM] * 3,
        HBM,
        [
            pltpu.SMEM(matching_lines.shape, jnp.int32),
            pltpu.VMEM(landed.shape, bf16),
            pltpu.VMEM((child_dev, BLK, 2 * HD), bf16),
            pltpu.VMEM((child_dev, BLK, 2 * HD), bf16),
            pltpu.SemaphoreType.DMA((2,)),
            pltpu.SemaphoreType.DMA((child_dev,)),
            pltpu.SemaphoreType.DMA((child_dev // GATHER,)),
        ],
        vmem=60,
        cost=(1000000, 8 * child_dev * BLK * 2 * HD, 0),
    )(matching_lines, all_tails.reshape(leaves, BLK, 2 * HD), landed)
    squares, children = lax.optimization_barrier((squares, children))
    branch = call(
        scale_kernel,
        shape((leaf_out, columns), bf16),
        [VMEM] * 3,
        VMEM,
    )(squares.reshape(nodes, HD), projected, post_gain.reshape(1, columns))
    return (branch, children.reshape(child_dev, BLK, 1, 2 * HD))


def solution(mesh):
    return jax.shard_map(
        shards,
        mesh=mesh,
        in_specs=(
            P(None, "node"),
            P("node", "head"),
            P("node", "head"),
            P("head", "node"),
            P("node"),
            P("node", None, "head", None),
            P("node", None, "head", None),
            P("node"),
            P(),
            P("node"),
            P(),
        ),
        out_specs=(P("head", "node"), P("node", None, "head", None)),
        check_vma=False,
    )
```
